128 devices in a mesh: row: 8 (over y, core), col: 16 (over z, x).
Axes of the slice: x: 4, y: 4, z: 4, core: 2. Of those that a mesh axis runs over, the one named last changes fastest.
Arguments:
- inputs: bfloat16 [1280, 6144], P('col', 'row'), may hold values from -6 to 6
- w_in: bfloat16 [6144, 24576], P('row', 'col'), may hold values from -0.078125 to 0.078125
- b_in: float32 [24576], P('col'), may hold values from -3 to 3
- w_out: bfloat16 [24576, 6144], P('col', 'row'), may hold values from -0.0390625 to 0.0390625
- b_out: float32 [6144], P('row'), may hold values from -3 to 3
- out_grad: bfloat16 [1280, 6144], P('col', 'row'), may hold values from -0.625 to 0.625
Outputs:
- output: bfloat16 [1280, 6144], P('col', 'row')
- input_grad: bfloat16 [1280, 6144], P('col', 'row')
- w_in_grad: float32 [6144, 24576], P('row', 'col')
- b_in_grad: float32 [24576], P('col')
- w_out_grad: float32 [24576, 6144], P('col', 'row')
- b_out_grad: float32 [6144], P('row')
The draws below stay inside these ranges and needn't reach their ends.
All inputs are finite; a program needn't handle non-finite values.
Results may differ from the reference program's by a relative error of at most 0.007.
Values may be sent and summed in bfloat16 or wider, within the bound.
A program may use at most 128 MiB of HBM per device.

```python
import jax
import jax.numpy as jnp

D = 6144
FF = 24576
TOKENS = 1280


def steps_of(stream_key, extent, shards, smallest, top_value):
    gain = 1.0
    for axis_at, shards_of in shards:
        heights = jax.random.uniform(jax.random.fold_in(jax.random.fold_in(stream_key, 6), axis_at), (shards_of,), jnp.float32, smallest / len(shards), top_value / len(shards))
        gain = gain * jnp.repeat(jnp.exp(heights), extent[axis_at] // shards_of).reshape((-1,) + (1,) * (len(extent) - 1 - axis_at))
    return gain


def bell_draw(stream_key, dims, deviation, bound, split=(), kind=jnp.bfloat16):
    result = jax.random.normal(stream_key, dims, jnp.float32) * deviation
    if len(split) > 0:
        result = steps_of(stream_key, dims, split, -0.22, 0.18) * result
    return jnp.clip(result, min=-bound, max=bound).astype(kind)


def setup_inputs(seed: int = 0) -> dict:
    streams_of = jax.random.split(jax.random.key(seed), 7)
    inputs = bell_draw(streams_of[0], (TOKENS, D), 1.0, 6.0, ((0, 16), (1, 8)))
    w_in = bell_draw(streams_of[1], (D, FF), D ** -0.5, 0.078125, ((0, 8), (1, 16)))
    b_in = bell_draw(streams_of[2], (FF,), 0.5, 3.0, ((0, 16),), jnp.float32)
    w_out = bell_draw(streams_of[3], (FF, D), FF ** -0.5, 0.0390625, ((0, 16), (1, 8)))
    b_out = bell_draw(streams_of[4], (D,), 0.5, 3.0, ((0, 8),), jnp.float32)
    out_grad = bell_draw(streams_of[5], (TOKENS, D), 0.1, 0.625, ((0, 16), (1, 8)))
    return {"inputs": inputs, "w_in": w_in, "b_in": b_in, "w_out": w_out, "b_out": b_out, "out_grad": out_grad}


def gelu_parts(hidden):
    half = 0.5 * (1.0 + jax.scipy.special.erf(hidden * 0.7071067811865476))
    slope = half + hidden * jnp.exp(-0.5 * hidden * hidden) * 0.3989422804014327
    return hidden * half, slope


def reference(inputs, w_in, b_in, w_out, b_out, out_grad):
    hidden = jnp.dot(inputs, w_in, preferred_element_type=jnp.float32) + b_in
    act, slope = gelu_parts(hidden)
    act = act.astype(jnp.bfloat16)
    output = (jnp.dot(act, w_out, preferred_element_type=jnp.float32) + b_out).astype(jnp.bfloat16)
    b_out_grad = jnp.sum(out_grad.astype(jnp.float32), axis=0)
    w_out_grad = jnp.dot(act.T, out_grad, preferred_element_type=jnp.float32)
    act_grad = jnp.dot(out_grad, w_out.T, preferred_element_type=jnp.float32)
    pre_grad = (act_grad * slope).astype(jnp.bfloat16)
    b_in_grad = jnp.sum(pre_grad.astype(jnp.float32), axis=0)
    w_in_grad = jnp.dot(inputs.T, pre_grad, preferred_element_type=jnp.float32)
    input_grad = jnp.dot(pre_grad, w_in.T, preferred_element_type=jnp.float32).astype(jnp.bfloat16)
    return (output, input_grad, w_in_grad, b_in_grad, w_out_grad, b_out_grad)
```

```python
import jax
import jax.numpy as jnp
from jax import lax
from jax.experimental import pallas as pl
from jax.experimental.pallas import tpu as pltpu
from jax.sharding import PartitionSpec as P

MESH = pl.DeviceIdType.MESH
BF16 = jnp.bfloat16
F32 = jnp.float32

CH = 5
TB = 16
ROWS = 256
HALF = ROWS // 2
DL = 768
FL = 1536
DH = DL // 2


def dot(a, b, dims):
    return lax.dot_general(a, b, ((dims[:1], dims[1:]), ((), ())), preferred_element_type=F32)


def body(
    x_hbm, g_hbm, w_in_hbm, w_out_hbm, b_in, b_out,
    out_o, out_i, out_w1, out_b1, out_w2, out_b2,
    xg, w_in, w_out, snd, crv, own, s, r1b, r2b, act, part, ra, rb, sa, sb, ta, tb, w1g, w2g, b1g, b2g,
    load_sem, ag1_s, ag1_r, ag2_s, ag2_r, ce_s, ce_r, y_s, y_r, gc_s, gc_r, rs1_s, rs1_r, rs2_s, rs2_r, st_sem,
):
    row, col = lax.axis_index("row"), lax.axis_index("col")
    y, core = row // 2, row % 2
    z, x = col // 4, col % 4
    abit, bbit = ((y + 1) // 2) % 2, y // 2
    ya, yb = y + 1 - 2 * (y % 2), 3 - y
    pair_a, pair_b = (ya * 2 + core, col), (yb * 2 + core, col)
    mate = (y * 2 + 1 - core, col)

    def zx(dz, dx):
        return (row, ((z + dz) % 4) * 4 + (x + dx) % 4)

    loads = [
        pltpu.make_async_copy(x_hbm, xg.at[:, 0, z, x], load_sem.at[0]),
        pltpu.make_async_copy(g_hbm, xg.at[:, 1, z, x], load_sem.at[1]),
        pltpu.make_async_copy(w_in_hbm, w_in, load_sem.at[2]),
        pltpu.make_async_copy(w_out_hbm, w_out, load_sem.at[3]),
    ]
    for cp in loads:
        cp.start()

    barrier = pltpu.get_barrier_semaphore()
    peers = [pair_a, pair_b, mate] + [zx(0, d) for d in (1, 2, 3)] + [zx(d, 0) for d in (1, 2, 3)]
    for p in peers:
        pl.semaphore_signal(barrier, inc=1, device_id=p, device_id_type=MESH)
    pl.semaphore_wait(barrier, len(peers))
    loads[0].wait()
    loads[1].wait()

    def rcopy(src, dst, ss, rs, dev):
        return pltpu.make_async_remote_copy(
            src_ref=src, dst_ref=dst, send_sem=ss, recv_sem=rs, device_id=dev, device_id_type=MESH
        )

    lo, hi = pl.ds(0, DH), pl.ds(DH, DH)

    def ag1(c):
        res = []
        for d in (1, 2, 3):
            ref = xg.at[c, :, z, x, :, lo]
            res.append(rcopy(ref, ref, ag1_s.at[c, d - 1], ag1_r.at[c, d - 1], zx(0, d)))
            ref = xg.at[c, :, z, x, :, hi]
            res.append(rcopy(ref, ref, ag1_s.at[c, d + 2], ag1_r.at[c, d + 2], zx(d, 0)))
        return res

    def ag2(c):
        res = []
        for d in (1, 2, 3):
            ref = xg.at[c, :, z, :, :, lo]
            res.append(rcopy(ref, ref, ag2_s.at[c, d - 1], ag2_r.at[c, d - 1], zx(d, 0)))
            ref = xg.at[c, :, :, x, :, hi]
            res.append(rcopy(ref, ref, ag2_s.at[c, d + 2], ag2_r.at[c, d + 2], zx(0, d)))
        return res

    def core_swap(c):
        return [rcopy(snd, crv.at[c], ce_s.at[c], ce_r.at[c], mate)]

    def rows(start, n):
        return pl.ds(pl.multiple_of(start, TB), n)

    a_keep, a_send = abit * 32, (1 - abit) * 32
    b_keep, b_send = 64 + bbit * 32, 64 + (1 - bbit) * 32
    a_own, a_send2 = a_keep + bbit * 16, a_keep + (1 - bbit) * 16
    b_own, b_send2 = b_keep + abit * 16, b_keep + (1 - abit) * 16

    def y_red1(c):
        return [
            rcopy(s.at[c, :, rows(a_send, 32)], r1b.at[c, 0], y_s.at[c, 0], y_r.at[c, 0], pair_a),
            rcopy(s.at[c, :, rows(b_send, 32)], r1b.at[c, 1], y_s.at[c, 1], y_r.at[c, 1], pair_b),
        ]

    def y_red2(c):
        return [
            rcopy(s.at[c, :, rows(a_send2, 16)], r2b.at[c, 0], y_s.at[c, 2], y_r.at[c, 2], pair_b),
            rcopy(s.at[c, :, rows(b_send2, 16)], r2b.at[c, 1], y_s.at[c, 3], y_r.at[c, 3], pair_a),
        ]

    def y_gat1(c):
        ref_a = act.at[c, :, rows(core * HALF + a_own, 16)]
        ref_b = act.at[c, :, rows(core * HALF + b_own, 16)]
        return [
            rcopy(ref_a, ref_a, y_s.at[c, 4], y_r.at[c, 4], pair_b),
            rcopy(ref_b, ref_b, y_s.at[c, 5], y_r.at[c, 5], pair_a),
        ]

    def y_gat2(c):
        ref_a = act.at[c, :, rows(core * HALF + a_keep, 32)]
        ref_b = act.at[c, :, rows(core * HALF + b_keep, 32)]
        return [
            rcopy(ref_a, ref_a, y_s.at[c, 6], y_r.at[c, 6], pair_a),
            rcopy(ref_b, ref_b, y_s.at[c, 7], y_r.at[c, 7], pair_b),
        ]

    def core_gat(c):
        ref = act.at[c, :, rows(core * HALF, HALF)]
        return [rcopy(ref, ref, gc_s.at[c], gc_r.at[c], mate)]

    def rs1(c):
        res = []
        for d in (1, 2, 3):
            src = part.at[c, :, :, (x + d) % 4, :, lo]
            res.append(rcopy(src, ra.at[c, d - 1], rs1_s.at[c, d - 1], rs1_r.at[c, d - 1], zx(0, d)))
            src = part.at[c, :, (z + d) % 4, :, :, hi]
            res.append(rcopy(src, rb.at[c, d - 1], rs1_s.at[c, d + 2], rs1_r.at[c, d + 2], zx(d, 0)))
        return res

    def rs2(c):
        res = []
        for d in (1, 2, 3):
            src = sa.at[c, :, (z + d) % 4]
            res.append(rcopy(src, ta.at[c, d - 1], rs2_s.at[c, d - 1], rs2_r.at[c, d - 1], zx(d, 0)))
            src = sb.at[c, :, (x + d) % 4]
            res.append(rcopy(src, tb.at[c, d - 1], rs2_s.at[c, d + 2], rs2_r.at[c, d + 2], zx(0, d)))
        return res

    def start(copies):
        for cp in copies:
            cp.start()

    def wait(copies):
        for cp in copies:
            cp.wait()

    w1g[...] = jnp.zeros_like(w1g)
    w2g[...] = jnp.zeros_like(w2g)
    b1g[...] = jnp.zeros_like(b1g)
    b2g[...] = jnp.zeros_like(b2g)

    def half_of(c, t, which):
        return xg[c, t, pl.ds(2 * which, 2)].reshape(HALF, DL)

    def chunk_of(c, t):
        return xg[c, t].reshape(ROWS, DL)

    @pl.loop(0, CH + 9)
    def _(i):
        def stage(offset, fn):
            c = i - offset
            pl.when(jnp.logical_and(c >= 0, c < CH))(lambda: fn(c))

        def red2_stage(c):
            wait(y_red1(c))
            for k, keep in ((0, a_keep), (1, b_keep)):
                here = s.at[c, :, rows(keep, 32)]
                here[...] = (here[...].astype(F32) + r1b[c, k].astype(F32)).astype(BF16)
            start(y_red2(c))

        def gelu_stage(c):
            wait(y_red2(c))
            for k, mine in ((0, a_own), (1, b_own)):
                total = s[c, :, rows(mine, 16)].astype(F32) + r2b[c, k].astype(F32)
                hidden = total[0] + b_in[...]
                half = 0.5 * (1.0 + lax.erf(hidden * 0.7071067811865476))
                slope = half + hidden * jnp.exp(-0.5 * hidden * hidden) * 0.3989422804014327
                at = rows(core * HALF + mine, 16)
                act[c, 0, at] = (hidden * half).astype(BF16)
                act[c, 1, at] = (total[1] * slope).astype(BF16)
            start(y_gat1(c))

        def gat2_stage(c):
            wait(y_gat1(c))
            start(y_gat2(c))

        def core_gat_stage(c):
            wait(y_gat2(c))
            start(core_gat(c))

        def ag1_stage(c):
            start(ag1(c))

        def ag2_stage(c):
            wait(ag1(c))
            start(ag2(c))

        def hidden_stage(c):
            @pl.when(c == 0)
            def _():
                loads[2].wait()
                loads[3].wait()

            wait(ag2(c))
            lhs = jnp.concatenate([half_of(c, 0, 1 - core), half_of(c, 0, core)], axis=0)
            for n in range(0, FL, 512):
                r = dot(lhs, w_in[:, n:n + 512], (1, 0))
                snd[0, :, n:n + 512] = r[:HALF].astype(BF16)
                own[0, :, n:n + 512] = r[HALF:]
            lhs = jnp.concatenate([half_of(c, 1, 1 - core), half_of(c, 1, core)], axis=0)
            for n in range(0, FL, 512):
                r = dot(lhs, w_out[n:n + 512, :], (1, 1))
                snd[1, :, n:n + 512] = r[:HALF].astype(BF16)
                own[1, :, n:n + 512] = r[HALF:]
            start(core_swap(c))

        def out_stage(c):
            wait(core_gat(c))
            for n in range(0, DL, 256):
                r = dot(act[c, 0], w_out[:, n:n + 256], (1, 0))
                part[c, 0, :, :, :, n:n + 256] = r.astype(BF16).reshape(4, 4, TB, 256)
            for n in range(0, DL, 256):
                r = dot(act[c, 1], w_in[n:n + 256, :], (1, 1))
                part[c, 1, :, :, :, n:n + 256] = r.astype(BF16).reshape(4, 4, TB, 256)
            start(rs1(c))

        def red1_stage(c):
            wait(core_swap(c))
            s[c] = (own[...] + crv[c].astype(F32)).astype(BF16)
            start(y_red1(c))

        def rs2_stage(c):
            wait(rs1(c))
            total = part[c, :, :, x, :, lo].astype(F32)
            for d in range(3):
                total += ra[c, d].astype(F32)
            sa[c] = total.astype(BF16)
            total = part[c, :, z, :, :, hi].astype(F32)
            for d in range(3):
                total += rb[c, d].astype(F32)
            sb[c] = total.astype(BF16)
            start(rs2(c))

        def final_stage(c):
            wait(rs2(c))
            for buf, got, me, cols in ((sa, ta, z, lo), (sb, tb, x, hi)):
                total = buf[c, :, me].astype(F32)
                for d in range(3):
                    total += got[c, d].astype(F32)
                out_o[c, :, cols] = (total[0] + b_out[:, cols]).astype(BF16)
                out_i[c, :, cols] = total[1].astype(BF16)

        def weight_stage(c):
            g_k = chunk_of(c, 1)
            for n in range(0, FL, 512):
                w2g[n:n + 512, :] += dot(act[c, 0, :, n:n + 512], g_k, (0, 0))
            x_k = chunk_of(c, 0)
            for n in range(0, FL, 512):
                w1g[:, n:n + 512] += dot(x_k, act[c, 1, :, n:n + 512], (0, 0))
            b1g[...] += jnp.sum(act[c, 1].astype(F32), axis=0, keepdims=True)
            b2g[...] += jnp.sum(g_k.astype(F32), axis=0, keepdims=True)

        stage(3, red2_stage)
        stage(4, gelu_stage)
        stage(5, gat2_stage)
        stage(6, core_gat_stage)
        stage(1, ag2_stage)
        stage(0, ag1_stage)
        stage(2, hidden_stage)
        stage(6, out_stage)
        stage(2, red1_stage)
        stage(7, rs2_stage)
        stage(8, final_stage)
        stage(6, weight_stage)

    stores = [
        pltpu.make_async_copy(w1g, out_w1, st_sem.at[0]),
        pltpu.make_async_copy(w2g, out_w2, st_sem.at[1]),
    ]
    for cp in stores:
        cp.start()
    out_b1[...] = b1g[...]
    out_b2[...] = b2g[...]
    for cp in stores:
        cp.wait()


def shards(inputs, w_in, b_in, w_out, b_out, out_grad):
    any_spec = pl.BlockSpec(memory_space=pl.ANY)
    vmem_spec = pl.BlockSpec(memory_space=pltpu.VMEM)
    dma = pltpu.SemaphoreType.DMA
    outs = pl.pallas_call(
        body,
        out_shape=[
            jax.ShapeDtypeStruct((CH, TB, DL), BF16),
            jax.ShapeDtypeStruct((CH, TB, DL), BF16),
            jax.ShapeDtypeStruct((DL, FL), F32),
            jax.ShapeDtypeStruct((1, FL), F32),
            jax.ShapeDtypeStruct((FL, DL), F32),
            jax.ShapeDtypeStruct((1, DL), F32),
        ],
        in_specs=[any_spec] * 4 + [vmem_spec] * 2,
        out_specs=[vmem_spec, vmem_spec, any_spec, vmem_spec, any_spec, vmem_spec],
        scratch_shapes=[
            pltpu.VMEM((CH, 2, 4, 4, TB, DL), BF16),
            pltpu.VMEM((DL, FL), BF16),
            pltpu.VMEM((FL, DL), BF16),
            pltpu.VMEM((2, HALF, FL), BF16),
            pltpu.VMEM((CH, 2, HALF, FL), BF16),
            pltpu.VMEM((2, HALF, FL), F32),
            pltpu.VMEM((CH, 2, HALF, FL), BF16),
            pltpu.VMEM((CH, 2, 2, 32, FL), BF16),
            pltpu.VMEM((CH, 2, 2, 16, FL), BF16),
            pltpu.VMEM((CH, 2, ROWS, FL), BF16),
            pltpu.VMEM((CH, 2, 4, 4, TB, DL), BF16),
            pltpu.VMEM((CH, 3, 2, 4, TB, DH), BF16),
            pltpu.VMEM((CH, 3, 2, 4, TB, DH), BF16),
            pltpu.VMEM((CH, 2, 4, TB, DH), BF16),
            pltpu.VMEM((CH, 2, 4, TB, DH), BF16),
            pltpu.VMEM((CH, 3, 2, TB, DH), BF16),
            pltpu.VMEM((CH, 3, 2, TB, DH), BF16),
            pltpu.VMEM((DL, FL), F32),
            pltpu.VMEM((FL, DL), F32),
            pltpu.VMEM((1, FL), F32),
            pltpu.VMEM((1, DL), F32),
            dma((4,)),
            dma((CH, 6)), dma((CH, 6)), dma((CH, 6)), dma((CH, 6)),
            dma((CH,)), dma((CH,)),
            dma((CH, 8)), dma((CH, 8)),
            dma((CH,)), dma((CH,)),
            dma((CH, 6)), dma((CH, 6)), dma((CH, 6)), dma((CH, 6)),
            dma((2,)),
        ],
        compiler_params=pltpu.CompilerParams(
            collective_id=0, has_side_effects=True, vmem_limit_bytes=60 * 2**20
        ),
        cost_estimate=pl.CostEstimate(flops=18 * 10**9, bytes_accessed=15 * 10**6, transcendentals=10**6),
        name="mlp",
    )(
        inputs.reshape(CH, TB, DL), out_grad.reshape(CH, TB, DL), w_in, w_out,
        b_in.reshape(1, FL), b_out.reshape(1, DL),
    )
    output, input_grad, w_in_grad, b_in_grad, w_out_grad, b_out_grad = outs
    return (
        output.reshape(CH * TB, DL), input_grad.reshape(CH * TB, DL),
        w_in_grad, b_in_grad.reshape(FL), w_out_grad, b_out_grad.reshape(DL),
    )


def solution(mesh):
    placed = (
        P("col", "row"),
        P("row", "col"),
        P("col"),
        P("col", "row"),
        P("row"),
        P("col", "row"),
    )
    return jax.shard_map(
        shards,
        mesh=mesh,
        in_specs=placed,
        out_specs=(
            P("col", "row"),
            P("col", "row"),
            P("row", "col"),
            P("col"),
            P("col", "row"),
            P("row"),
        ),
        check_vma=False,
    )
```

```python
import jax
import jax.numpy as jnp
from jax import lax
from jax.experimental import pallas as pl
from jax.experimental.pallas import tpu as pltpu
from jax.sharding import PartitionSpec as P

MESH = pl.DeviceIdType.MESH
BF16 = jnp.bfloat16
F32 = jnp.float32

CH = 5
TB = 16
ROWS = 256
HALF = ROWS // 2
DL = 768
FL = 1536
DH = DL // 2


def dot(a, b, dims):
    return lax.dot_general(a, b, ((dims[:1], dims[1:]), ((), ())), preferred_element_type=F32)


def body(
    x_hbm, g_hbm, w_in_hbm, w_out_hbm, b_in, b_out,
    out_o, out_i, w1g, out_b1, w2g, out_b2,
    xg, w_in, w_out, snd, crv, own, s, r1b, r2b, act, part, ra, rb, sa, sb, ta, tb, b1g, b2g,
    load_sem, ag1_s, ag1_r, ag2_s, ag2_r, ce_s, ce_r, y_s, y_r, gc_s, gc_r, rs1_s, rs1_r, rs2_s, rs2_r,
):
    row, col = lax.axis_index("row"), lax.axis_index("col")
    y, core = row // 2, row % 2
    z, x = col // 4, col % 4
    abit, bbit = ((y + 1) // 2) % 2, y // 2
    ya, yb = y + 1 - 2 * (y % 2), 3 - y
    pair_a, pair_b = (ya * 2 + core, col), (yb * 2 + core, col)
    mate = (y * 2 + 1 - core, col)

    def zx(dz, dx):
        return (row, ((z + dz) % 4) * 4 + (x + dx) % 4)

    loads = [
        pltpu.make_async_copy(x_hbm, xg.at[:, 0, z, x], load_sem.at[0]),
        pltpu.make_async_copy(g_hbm, xg.at[:, 1, z, x], load_sem.at[1]),
        pltpu.make_async_copy(w_in_hbm, w_in, load_sem.at[2]),
        pltpu.make_async_copy(w_out_hbm, w_out, load_sem.at[3]),
    ]
    for cp in loads:
        cp.start()

    barrier = pltpu.get_barrier_semaphore()
    peers = [pair_a, pair_b, mate] + [zx(0, d) for d in (1, 2, 3)] + [zx(d, 0) for d in (1, 2, 3)]
    for p in peers:
        pl.semaphore_signal(barrier, inc=1, device_id=p, device_id_type=MESH)
    pl.semaphore_wait(barrier, len(peers))
    loads[0].wait()
    loads[1].wait()

    def rcopy(src, dst, ss, rs, dev):
        return pltpu.make_async_remote_copy(
            src_ref=src, dst_ref=dst, send_sem=ss, recv_sem=rs, device_id=dev, device_id_type=MESH
        )

    lo, hi = pl.ds(0, DH), pl.ds(DH, DH)

    def ag1(c):
        res = []
        for d in (1, 2, 3):
            ref = xg.at[c, :, z, x, :, lo]
            res.append(rcopy(ref, ref, ag1_s.at[c, d - 1], ag1_r.at[c, d - 1], zx(0, d)))
            ref = xg.at[c, :, z, x, :, hi]
            res.append(rcopy(ref, ref, ag1_s.at[c, d + 2], ag1_r.at[c, d + 2], zx(d, 0)))
        return res

    def ag2(c):
        res = []
        for d in (1, 2, 3):
            ref = xg.at[c, :, z, :, :, lo]
            res.append(rcopy(ref, ref, ag2_s.at[c, d - 1], ag2_r.at[c, d - 1], zx(d, 0)))
            ref = xg.at[c, :, :, x, :, hi]
            res.append(rcopy(ref, ref, ag2_s.at[c, d + 2], ag2_r.at[c, d + 2], zx(0, d)))
        return res

    def core_swap(c):
        return [rcopy(snd, crv.at[c], ce_s.at[c], ce_r.at[c], mate)]

    def rows(start, n):
        return pl.ds(pl.multiple_of(start, TB), n)

    a_keep, a_send = abit * 32, (1 - abit) * 32
    b_keep, b_send = 64 + bbit * 32, 64 + (1 - bbit) * 32
    a_own, a_send2 = a_keep + bbit * 16, a_keep + (1 - bbit) * 16
    b_own, b_send2 = b_keep + abit * 16, b_keep + (1 - abit) * 16

    def y_red1(c):
        return [
            rcopy(s.at[c, :, rows(a_send, 32)], r1b.at[c, 0], y_s.at[c, 0], y_r.at[c, 0], pair_a),
            rcopy(s.at[c, :, rows(b_send, 32)], r1b.at[c, 1], y_s.at[c, 1], y_r.at[c, 1], pair_b),
        ]

    def y_red2(c):
        return [
            rcopy(s.at[c, :, rows(a_send2, 16)], r2b.at[c, 0], y_s.at[c, 2], y_r.at[c, 2], pair_b),
            rcopy(s.at[c, :, rows(b_send2, 16)], r2b.at[c, 1], y_s.at[c, 3], y_r.at[c, 3], pair_a),
        ]

    def y_gat1(c):
        ref_a = act.at[c, :, rows(core * HALF + a_own, 16)]
        ref_b = act.at[c, :, rows(core * HALF + b_own, 16)]
        return [
            rcopy(ref_a, ref_a, y_s.at[c, 4], y_r.at[c, 4], pair_b),
            rcopy(ref_b, ref_b, y_s.at[c, 5], y_r.at[c, 5], pair_a),
        ]

    def y_gat2(c):
        ref_a = act.at[c, :, rows(core * HALF + a_keep, 32)]
        ref_b = act.at[c, :, rows(core * HALF + b_keep, 32)]
        return [
            rcopy(ref_a, ref_a, y_s.at[c, 6], y_r.at[c, 6], pair_a),
            rcopy(ref_b, ref_b, y_s.at[c, 7], y_r.at[c, 7], pair_b),
        ]

    def core_gat(c):
        ref = act.at[c, :, rows(core * HALF, HALF)]
        return [rcopy(ref, ref, gc_s.at[c], gc_r.at[c], mate)]

    def rs1(c):
        res = []
        for d in (1, 2, 3):
            src = part.at[c, :, :, (x + d) % 4, :, lo]
            res.append(rcopy(src, ra.at[c, d - 1], rs1_s.at[c, d - 1], rs1_r.at[c, d - 1], zx(0, d)))
            src = part.at[c, :, (z + d) % 4, :, :, hi]
            res.append(rcopy(src, rb.at[c, d - 1], rs1_s.at[c, d + 2], rs1_r.at[c, d + 2], zx(d, 0)))
        return res

    def rs2(c):
        res = []
        for d in (1, 2, 3):
            src = sa.at[c, :, (z + d) % 4]
            res.append(rcopy(src, ta.at[c, d - 1], rs2_s.at[c, d - 1], rs2_r.at[c, d - 1], zx(d, 0)))
            src = sb.at[c, :, (x + d) % 4]
            res.append(rcopy(src, tb.at[c, d - 1], rs2_s.at[c, d + 2], rs2_r.at[c, d + 2], zx(0, d)))
        return res

    def start(copies):
        for cp in copies:
            cp.start()

    def wait(copies):
        for cp in copies:
            cp.wait()

    w1g[...] = jnp.zeros_like(w1g)
    w2g[...] = jnp.zeros_like(w2g)
    b1g[...] = jnp.zeros_like(b1g)
    b2g[...] = jnp.zeros_like(b2g)

    def half_of(c, t, which):
        return xg[c, t, pl.ds(2 * which, 2)].reshape(HALF, DL)

    def chunk_of(c, t):
        return xg[c, t].reshape(ROWS, DL)

    @pl.loop(0, CH + 9)
    def _(i):
        def stage(offset, fn):
            c = i - offset
            pl.when(jnp.logical_and(c >= 0, c < CH))(lambda: fn(c))

        def red2_stage(c):
            wait(y_red1(c))
            for k, keep in ((0, a_keep), (1, b_keep)):
                here = s.at[c, :, rows(keep, 32)]
                here[...] = (here[...].astype(F32) + r1b[c, k].astype(F32)).astype(BF16)
            start(y_red2(c))

        def gelu_stage(c):
            wait(y_red2(c))
            for k, mine in ((0, a_own), (1, b_own)):
                total = s[c, :, rows(mine, 16)].astype(F32) + r2b[c, k].astype(F32)
                hidden = total[0] + b_in[...][None]
                half = 0.5 * (1.0 + lax.erf(hidden * 0.7071067811865476))
                slope = half + hidden * jnp.exp(-0.5 * hidden * hidden) * 0.3989422804014327
                at = rows(core * HALF + mine, 16)
                act[c, 0, at] = (hidden * half).astype(BF16)
                act[c, 1, at] = (total[1] * slope).astype(BF16)
            start(y_gat1(c))

        def gat2_stage(c):
            wait(y_gat1(c))
            start(y_gat2(c))

        def core_gat_stage(c):
            wait(y_gat2(c))
            start(core_gat(c))

        def ag1_stage(c):
            start(ag1(c))

        def ag2_stage(c):
            wait(ag1(c))
            start(ag2(c))

        def hidden_stage(c):
            @pl.when(c == 0)
            def _():
                loads[2].wait()
                loads[3].wait()

            wait(ag2(c))
            lhs = jnp.concatenate([half_of(c, 0, 1 - core), half_of(c, 0, core)], axis=0)
            for n in range(0, FL, 512):
                r = dot(lhs, w_in[:, n:n + 512], (1, 0))
                snd[0, :, n:n + 512] = r[:HALF].astype(BF16)
                own[0, :, n:n + 512] = r[HALF:]
            lhs = jnp.concatenate([half_of(c, 1, 1 - core), half_of(c, 1, core)], axis=0)
            for n in range(0, FL, 512):
                r = dot(lhs, w_out[n:n + 512, :], (1, 1))
                snd[1, :, n:n + 512] = r[:HALF].astype(BF16)
                own[1, :, n:n + 512] = r[HALF:]
            start(core_swap(c))

        def out_stage(c):
            wait(core_gat(c))
            for n in range(0, DL, 256):
                r = dot(act[c, 0], w_out[:, n:n + 256], (1, 0))
                part[c, 0, :, :, :, n:n + 256] = r.astype(BF16).reshape(4, 4, TB, 256)
            for n in range(0, DL, 256):
                r = dot(act[c, 1], w_in[n:n + 256, :], (1, 1))
                part[c, 1, :, :, :, n:n + 256] = r.astype(BF16).reshape(4, 4, TB, 256)
            start(rs1(c))

        def red1_stage(c):
            wait(core_swap(c))
            s[c] = (own[...] + crv[c].astype(F32)).astype(BF16)
            start(y_red1(c))

        def rs2_stage(c):
            wait(rs1(c))
            total = part[c, :, :, x, :, lo].astype(F32)
            for d in range(3):
                total += ra[c, d].astype(F32)
            sa[c] = total.astype(BF16)
            total = part[c, :, z, :, :, hi].astype(F32)
            for d in range(3):
                total += rb[c, d].astype(F32)
            sb[c] = total.astype(BF16)
            start(rs2(c))

        def final_stage(c):
            wait(rs2(c))
            for buf, got, me, cols in ((sa, ta, z, lo), (sb, tb, x, hi)):
                total = buf[c, :, me].astype(F32)
                for d in range(3):
                    total += got[c, d].astype(F32)
                out_o[c, :, cols] = (total[0] + b_out[cols][None]).astype(BF16)
                out_i[c, :, cols] = total[1].astype(BF16)

        def weight_stage(c):
            g_k = chunk_of(c, 1)
            for n in range(0, FL, 512):
                w2g[n:n + 512, :] += dot(act[c, 0, :, n:n + 512], g_k, (0, 0))
            x_k = chunk_of(c, 0)
            for n in range(0, FL, 512):
                w1g[:, n:n + 512] += dot(x_k, act[c, 1, :, n:n + 512], (0, 0))
            b1g[...] += jnp.sum(act[c, 1].astype(F32), axis=0, keepdims=True)
            b2g[...] += jnp.sum(g_k.astype(F32), axis=0, keepdims=True)

        stage(6, gat2_stage)
        stage(5, gelu_stage)
        stage(4, red2_stage)
        stage(3, red1_stage)
        stage(7, core_gat_stage)
        stage(1, ag2_stage)
        stage(0, ag1_stage)
        stage(2, hidden_stage)
        stage(9, final_stage)
        stage(8, rs2_stage)
        stage(7, out_stage)
        stage(7, weight_stage)

    out_b1[...] = jnp.sum(b1g[...], axis=0)
    out_b2[...] = jnp.sum(b2g[...], axis=0)


def write_out(*refs):
    sems = refs[-1]
    copies = [pltpu.make_async_copy(refs[k], refs[k + 6], sems.at[k]) for k in range(6)]
    for cp in copies:
        cp.start()
    for cp in copies:
        cp.wait()


def shards(inputs, w_in, b_in, w_out, b_out, out_grad):
    any_spec = pl.BlockSpec(memory_space=pl.ANY)
    vmem_spec = pl.BlockSpec(memory_space=pltpu.VMEM)
    dma = pltpu.SemaphoreType.DMA
    outs = pl.pallas_call(
        body,
        out_shape=[
            pltpu.VMEM((CH, TB, DL), BF16),
            pltpu.VMEM((CH, TB, DL), BF16),
            pltpu.VMEM((DL, FL), F32),
            pltpu.VMEM((FL,), F32),
            pltpu.VMEM((FL, DL), F32),
            pltpu.VMEM((DL,), F32),
        ],
        in_specs=[any_spec] * 4 + [vmem_spec] * 2,
        out_specs=[vmem_spec] * 6,
        scratch_shapes=[
            pltpu.VMEM((CH, 2, 4, 4, TB, DL), BF16),
            pltpu.VMEM((DL, FL), BF16),
            pltpu.VMEM((FL, DL), BF16),
            pltpu.VMEM((2, HALF, FL), BF16),
            pltpu.VMEM((CH, 2, HALF, FL), BF16),
            pltpu.VMEM((2, HALF, FL), F32),
            pltpu.VMEM((CH, 2, HALF, FL), BF16),
            pltpu.VMEM((CH, 2, 2, 32, FL), BF16),
            pltpu.VMEM((CH, 2, 2, 16, FL), BF16),
            pltpu.VMEM((CH, 2, ROWS, FL), BF16),
            pltpu.VMEM((CH, 2, 4, 4, TB, DL), BF16),
            pltpu.VMEM((CH, 3, 2, 4, TB, DH), BF16),
            pltpu.VMEM((CH, 3, 2, 4, TB, DH), BF16),
            pltpu.VMEM((CH, 2, 4, TB, DH), BF16),
            pltpu.VMEM((CH, 2, 4, TB, DH), BF16),
            pltpu.VMEM((CH, 3, 2, TB, DH), BF16),
            pltpu.VMEM((CH, 3, 2, TB, DH), BF16),
            pltpu.VMEM((1, FL), F32),
            pltpu.VMEM((1, DL), F32),
            dma((4,)),
            dma((CH, 6)), dma((CH, 6)), dma((CH, 6)), dma((CH, 6)),
            dma((CH,)), dma((CH,)),
            dma((CH, 8)), dma((CH, 8)),
            dma((CH,)), dma((CH,)),
            dma((CH, 6)), dma((CH, 6)), dma((CH, 6)), dma((CH, 6)),
        ],
        compiler_params=pltpu.CompilerParams(
            collective_id=0, has_side_effects=True, vmem_limit_bytes=48 * 2**20
        ),
        cost_estimate=pl.CostEstimate(flops=18 * 10**9, bytes_accessed=15 * 10**6, transcendentals=10**6),
        name="mlp",
    )(
        inputs.reshape(CH, TB, DL), out_grad.reshape(CH, TB, DL), w_in, w_out,
        b_in, b_out,
    )
    outs = pl.pallas_call(
        write_out,
        out_shape=[jax.ShapeDtypeStruct(o.shape, o.dtype) for o in outs],
        in_specs=[vmem_spec] * 6,
        out_specs=[any_spec] * 6,
        scratch_shapes=[dma((6,))],
        compiler_params=pltpu.CompilerParams(vmem_limit_bytes=2**20),
        name="write_out",
    )(*[pltpu.with_memory_space_constraint(o, pltpu.VMEM) for o in outs])
    output, input_grad, *grads = outs
    return output.reshape(CH * TB, DL), input_grad.reshape(CH * TB, DL), *grads


def solution(mesh):
    placed = (
        P("col", "row"),
        P("row", "col"),
        P("col"),
        P("col", "row"),
        P("row"),
        P("col", "row"),
    )
    return jax.shard_map(
        shards,
        mesh=mesh,
        in_specs=placed,
        out_specs=(
            P("col", "row"),
            P("col", "row"),
            P("row", "col"),
            P("col"),
            P("col", "row"),
            P("row"),
        ),
        check_vma=False,
    )
```

```python
import jax
import jax.numpy as jnp
from jax import lax
from jax.experimental import pallas as pl
from jax.experimental.pallas import tpu as pltpu
from jax.sharding import PartitionSpec as P

MESH = pl.DeviceIdType.MESH
BF16 = jnp.bfloat16
F32 = jnp.float32

CH = 5
TB = 16
ROWS = 256
HALF = ROWS // 2
DL = 768
FL = 1536
DH = DL // 2


def dot(a, b, dims):
    return lax.dot_general(a, b, ((dims[:1], dims[1:]), ((), ())), preferred_element_type=F32)


def body(
    x_hbm, g_hbm, w_in_hbm, w_out_hbm, b_in_hbm, b_out_hbm,
    out_o, out_i, w1g, out_b1, w2g, out_b2,
    xg, w_in, w_out, snd, crv, own, s, r1b, r2b, act, part, rab, sab, tab, b1g, b2g, b_in, b_out,
    load_sem, ag1_s, ag1_r, ag2_s, ag2_r, ce_s, ce_r, y_s, y_r, gc_s, gc_r, rs1_s, rs1_r, rs2_s, rs2_r,
):
    row, col = lax.axis_index("row"), lax.axis_index("col")
    y, core = row // 2, row % 2
    z, x = col // 4, col % 4
    abit, bbit = ((y + 1) // 2) % 2, y // 2
    ya, yb = y + 1 - 2 * (y % 2), 3 - y
    pair_a, pair_b = (ya * 2 + core, col), (yb * 2 + core, col)
    mate = (y * 2 + 1 - core, col)

    def zx(dz, dx):
        return (row, ((z + dz) % 4) * 4 + (x + dx) % 4)

    loads = [
        pltpu.make_async_copy(x_hbm, xg.at[:, 0, z, x], load_sem.at[0]),
        pltpu.make_async_copy(g_hbm, xg.at[:, 1, z, x], load_sem.at[1]),
        pltpu.make_async_copy(w_in_hbm, w_in, load_sem.at[2]),
        pltpu.make_async_copy(w_out_hbm, w_out, load_sem.at[3]),
        pltpu.make_async_copy(b_in_hbm, b_in, load_sem.at[4]),
        pltpu.make_async_copy(b_out_hbm, b_out, load_sem.at[5]),
    ]
    for cp in loads:
        cp.start()

    barrier = pltpu.get_barrier_semaphore()
    peers = [pair_a, pair_b, mate] + [zx(0, d) for d in (1, 2, 3)] + [zx(d, 0) for d in (1, 2, 3)]
    for p in peers:
        pl.semaphore_signal(barrier, inc=1, device_id=p, device_id_type=MESH)
    pl.semaphore_wait(barrier, len(peers))
    loads[0].wait()
    loads[1].wait()

    def rcopy(src, dst, ss, rs, dev):
        return lambda: pltpu.make_async_remote_copy(
            src_ref=src, dst_ref=dst, send_sem=ss, recv_sem=rs, device_id=dev, device_id_type=MESH
        ).start()

    lo, hi = pl.ds(0, DH), pl.ds(DH, DH)

    def ag1(c):
        ss, rs = ag1_s.at[c % 2], ag1_r.at[c]
        res = []
        for d in (1, 2, 3):
            ref = xg.at[c, :, z, x, :, lo]
            res.append(rcopy(ref, ref, ss, rs, zx(0, d)))
            ref = xg.at[c, :, z, x, :, hi]
            res.append(rcopy(ref, ref, ss, rs, zx(d, 0)))
        return res, xg.at[c, :, 0, 0:3], ss, rs

    def ag2(c, t):
        ss, rs = ag2_s.at[c % 2, t], ag2_r.at[c, t]
        res = []
        for d in (1, 2, 3):
            ref = xg.at[c, t, z, :, :, lo]
            res.append(rcopy(ref, ref, ss, rs, zx(d, 0)))
            ref = xg.at[c, t, :, x, :, hi]
            res.append(rcopy(ref, ref, ss, rs, zx(0, d)))
        return res, xg.at[c, t, 0:3], ss, rs

    def core_swap(c, t):
        ss, rs = ce_s.at[c % 2, t], ce_r.at[c, t]
        return [rcopy(snd.at[t], crv.at[c, t], ss, rs, mate)], crv.at[c, t], ss, rs

    def rows(start, n):
        return pl.ds(pl.multiple_of(start, TB), n)

    a_keep, a_send = abit * 32, (1 - abit) * 32
    b_keep, b_send = 64 + bbit * 32, 64 + (1 - bbit) * 32
    a_own, a_send2 = a_keep + bbit * 16, a_keep + (1 - bbit) * 16
    b_own, b_send2 = b_keep + abit * 16, b_keep + (1 - abit) * 16

    def y_red1(c, t):
        ss, rs = y_s.at[c % 2, t, 0], y_r.at[c, t, 0]
        return [
            rcopy(s.at[c, t, rows(a_send, 32)], r1b.at[c, t, 0], ss, rs, pair_a),
            rcopy(s.at[c, t, rows(b_send, 32)], r1b.at[c, t, 1], ss, rs, pair_b),
        ], r1b.at[c, t], ss, rs

    def y_red2(c, t):
        ss, rs = y_s.at[c % 2, t, 1], y_r.at[c, t, 1]
        return [
            rcopy(s.at[c, t, rows(a_send2, 16)], r2b.at[c, t, 0], ss, rs, pair_b),
            rcopy(s.at[c, t, rows(b_send2, 16)], r2b.at[c, t, 1], ss, rs, pair_a),
        ], r2b.at[c, t], ss, rs

    def y_gat1(c, t):
        ss, rs = y_s.at[c % 2, t, 2], y_r.at[c, t, 2]
        ref_a = act.at[c, t, rows(core * HALF + a_own, 16)]
        ref_b = act.at[c, t, rows(core * HALF + b_own, 16)]
        return [rcopy(ref_a, ref_a, ss, rs, pair_b), rcopy(ref_b, ref_b, ss, rs, pair_a)], act.at[c, t, 0:32], ss, rs

    def y_gat2(c, t):
        ss, rs = y_s.at[c % 2, t, 3], y_r.at[c, t, 3]
        ref_a = act.at[c, t, rows(core * HALF + a_keep, 32)]
        ref_b = act.at[c, t, rows(core * HALF + b_keep, 32)]
        return [rcopy(ref_a, ref_a, ss, rs, pair_a), rcopy(ref_b, ref_b, ss, rs, pair_b)], act.at[c, t, 0:64], ss, rs

    def core_gat(c, t):
        ss, rs = gc_s.at[c % 2, t], gc_r.at[c, t]
        ref = act.at[c, t, rows(core * HALF, HALF)]
        return [rcopy(ref, ref, ss, rs, mate)], ref, ss, rs

    def rs1(c, t):
        ss, rs = rs1_s.at[c % 2, t], rs1_r.at[c, t]
        res = []
        for d in (1, 2, 3):
            src = part.at[c, t, :, (x + d) % 4, :, lo]
            res.append(rcopy(src, rab.at[c, t, 0, d - 1], ss, rs, zx(0, d)))
            src = part.at[c, t, (z + d) % 4, :, :, hi]
            res.append(rcopy(src, rab.at[c, t, 1, d - 1], ss, rs, zx(d, 0)))
        return res, rab.at[c, t], ss, rs

    def rs2(c):
        ss, rs = rs2_s.at[c % 2], rs2_r.at[c]
        res = []
        for d in (1, 2, 3):
            src = sab.at[c, 0, :, (z + d) % 4]
            res.append(rcopy(src, tab.at[c, 0, d - 1], ss, rs, zx(d, 0)))
            src = sab.at[c, 1, :, (x + d) % 4]
            res.append(rcopy(src, tab.at[c, 1, d - 1], ss, rs, zx(0, d)))
        return res, tab.at[c], ss, rs

    def start(stage):
        for send in stage[0]:
            send()

    def wait(stage):
        _, size, ss, rs = stage
        pltpu.make_async_copy(size, size, rs).wait()
        pltpu.make_async_copy(size, size, ss).wait()

    def half_of(c, t, which):
        return xg[c, t, pl.ds(2 * which, 2)].reshape(HALF, DL)

    def chunk_of(c, t):
        return xg[c, t].reshape(ROWS, DL)

    @pl.loop(0, CH + 9)
    def _(i):
        def stage(offset, fn):
            c = i - offset
            pl.when(jnp.logical_and(c >= 0, c < CH))(lambda: fn(c))

        def red2_stage(t):
            def run(c):
                wait(y_red1(c, t))
                for k, keep in ((0, a_keep), (1, b_keep)):
                    here = s.at[c, t, rows(keep, 32)]
                    here[...] = (here[...].astype(F32) + r1b[c, t, k].astype(F32)).astype(BF16)
                start(y_red2(c, t))

            return run

        def gelu_stage(c):
            wait(y_red2(c, 0))
            wait(y_red2(c, 1))
            for k, mine in ((0, a_own), (1, b_own)):
                total = s[c, :, rows(mine, 16)].astype(F32) + r2b[c, :, k].astype(F32)
                hidden = total[0] + b_in[...][None]
                half = 0.5 * (1.0 + lax.erf(hidden * 0.7071067811865476))
                slope = half + hidden * jnp.exp(-0.5 * hidden * hidden) * 0.3989422804014327
                at = rows(core * HALF + mine, 16)
                act[c, 0, at] = (hidden * half).astype(BF16)
                act[c, 1, at] = (total[1] * slope).astype(BF16)
            start(y_gat1(c, 0))
            start(y_gat1(c, 1))

        def gat2_stage(t):
            def run(c):
                wait(y_gat1(c, t))
                start(y_gat2(c, t))

            return run

        def core_gat_stage(t):
            def run(c):
                wait(y_gat2(c, t))
                start(core_gat(c, t))

            return run

        def ag1_stage(c):
            start(ag1(c))

        def ag2_stage(c):
            wait(ag1(c))
            start(ag2(c, 0))
            start(ag2(c, 1))

        def hidden_stage(t):
            def run(c):
                @pl.when(c == 0)
                def _():
                    loads[2 + t].wait()
                    loads[4 + t].wait()

                wait(ag2(c, t))
                lhs = jnp.concatenate([half_of(c, t, 1 - core), half_of(c, t, core)], axis=0)
                for n in range(0, FL, 512):
                    if t == 0:
                        r = dot(lhs, w_in[:, n:n + 512], (1, 0))
                    else:
                        r = dot(lhs, w_out[n:n + 512, :], (1, 1))
                    snd[t, :, n:n + 512] = r[:HALF].astype(BF16)
                    own[t, :, n:n + 512] = r[HALF:]
                start(core_swap(c, t))

            return run

        def out_stage(t):
            def run(c):
                wait(core_gat(c, t))
                for n in range(0, DL, 256):
                    if t == 0:
                        r = dot(act[c, 0], w_out[:, n:n + 256], (1, 0))
                    else:
                        r = dot(act[c, 1], w_in[n:n + 256, :], (1, 1))
                    part[c, t, :, :, :, n:n + 256] = r.astype(BF16).reshape(4, 4, TB, 256)
                start(rs1(c, t))

            return run

        def red1_stage(t):
            def run(c):
                wait(core_swap(c, t))
                s[c, t] = (own[t] + crv[c, t].astype(F32)).astype(BF16)
                start(y_red1(c, t))

            return run

        def rs2_stage(c):
            for t in (0, 1):
                wait(rs1(c, t))
                total = part[c, t, :, x, :, lo].astype(F32)
                for d in range(3):
                    total += rab[c, t, 0, d].astype(F32)
                sab[c, 0, t] = total.astype(BF16)
                total = part[c, t, z, :, :, hi].astype(F32)
                for d in range(3):
                    total += rab[c, t, 1, d].astype(F32)
                sab[c, 1, t] = total.astype(BF16)
            start(rs2(c))

        def final_stage(c):
            wait(rs2(c))
            for k, me, cols in ((0, z, lo), (1, x, hi)):
                total = sab[c, k, :, me].astype(F32)
                for d in range(3):
                    total += tab[c, k, d].astype(F32)
                out_o[c, :, cols] = (total[0] + b_out[cols][None]).astype(BF16)
                out_i[c, :, cols] = total[1].astype(BF16)

        def weight_stage(c):
            g_k = chunk_of(c, 1)
            for n in range(0, FL, 512):
                w2g[n:n + 512, :] += dot(act[c, 0, :, n:n + 512], g_k, (0, 0))
            x_k = chunk_of(c, 0)
            for n in range(0, FL, 512):
                w1g[:, n:n + 512] += dot(x_k, act[c, 1, :, n:n + 512], (0, 0))
            b1g[...] += jnp.sum(act[c, 1].astype(F32), axis=0, keepdims=True)
            b2g[...] += jnp.sum(g_k.astype(F32), axis=0, keepdims=True)

        def zero_stage(c):
            @pl.when(c == 0)
            def _():
                w1g[...] = jnp.zeros_like(w1g)
                w2g[...] = jnp.zeros_like(w2g)
                b1g[...] = jnp.zeros_like(b1g)
                b2g[...] = jnp.zeros_like(b2g)

        stage(6, gat2_stage(0))
        stage(4, red2_stage(0))
        stage(3, red1_stage(0))
        stage(5, gelu_stage)
        stage(6, gat2_stage(1))
        stage(4, red2_stage(1))
        stage(3, red1_stage(1))
        stage(7, core_gat_stage(0))
        stage(1, ag2_stage)
        stage(0, ag1_stage)
        stage(1, zero_stage)
        stage(2, hidden_stage(0))
        stage(7, core_gat_stage(1))
        stage(7, out_stage(0))
        stage(2, hidden_stage(1))
        stage(7, out_stage(1))
        stage(9, final_stage)
        stage(8, rs2_stage)
        stage(7, weight_stage)

    out_b1[...] = jnp.sum(b1g[...], axis=0)
    out_b2[...] = jnp.sum(b2g[...], axis=0)


def write_out(*refs):
    sems = refs[-1]
    copies = [pltpu.make_async_copy(refs[k], refs[k + 6], sems.at[k]) for k in range(6)]
    for cp in copies:
        cp.start()
    for cp in copies:
        cp.wait()


def shards(inputs, w_in, b_in, w_out, b_out, out_grad):
    any_spec = pl.BlockSpec(memory_space=pl.ANY)
    vmem_spec = pl.BlockSpec(memory_space=pltpu.VMEM)
    dma = pltpu.SemaphoreType.DMA
    outs = pl.pallas_call(
        body,
        out_shape=[
            pltpu.VMEM((CH, TB, DL), BF16),
            pltpu.VMEM((CH, TB, DL), BF16),
            pltpu.VMEM((DL, FL), F32),
            pltpu.VMEM((FL,), F32),
            pltpu.VMEM((FL, DL), F32),
            pltpu.VMEM((DL,), F32),
        ],
        in_specs=[any_spec] * 6,
        out_specs=[vmem_spec] * 6,
        scratch_shapes=[
            pltpu.VMEM((CH, 2, 4, 4, TB, DL), BF16),
            pltpu.VMEM((DL, FL), BF16),
            pltpu.VMEM((FL, DL), BF16),
            pltpu.VMEM((2, HALF, FL), BF16),
            pltpu.VMEM((CH, 2, HALF, FL), BF16),
            pltpu.VMEM((2, HALF, FL), F32),
            pltpu.VMEM((CH, 2, HALF, FL), BF16),
            pltpu.VMEM((CH, 2, 2, 32, FL), BF16),
            pltpu.VMEM((CH, 2, 2, 16, FL), BF16),
            pltpu.VMEM((CH, 2, ROWS, FL), BF16),
            pltpu.VMEM((CH, 2, 4, 4, TB, DL), BF16),
            pltpu.VMEM((CH, 2, 2, 3, 4, TB, DH), BF16),
            pltpu.VMEM((CH, 2, 2, 4, TB, DH), BF16),
            pltpu.VMEM((CH, 2, 3, 2, TB, DH), BF16),
            pltpu.VMEM((1, FL), F32),
            pltpu.VMEM((1, DL), F32),
            pltpu.VMEM((FL,), F32),
            pltpu.VMEM((DL,), F32),
            dma((6,)),
            dma((2,)), dma((CH,)), dma((2, 2)), dma((CH, 2)),
            dma((2, 2)), dma((CH, 2)),
            dma((2, 2, 4)), dma((CH, 2, 4)),
            dma((2, 2)), dma((CH, 2)),
            dma((2, 2)), dma((CH, 2)), dma((2,)), dma((CH,)),
        ],
        compiler_params=pltpu.CompilerParams(
            collective_id=0, has_side_effects=True, vmem_limit_bytes=48 * 2**20
        ),
        cost_estimate=pl.CostEstimate(flops=18 * 10**9, bytes_accessed=15 * 10**6, transcendentals=10**6),
        name="mlp",
    )(
        inputs.reshape(CH, TB, DL), out_grad.reshape(CH, TB, DL), w_in, w_out,
        b_in, b_out,
    )
    outs = pl.pallas_call(
        write_out,
        out_shape=[jax.ShapeDtypeStruct(o.shape, o.dtype) for o in outs],
        in_specs=[vmem_spec] * 6,
        out_specs=[any_spec] * 6,
        scratch_shapes=[dma((6,))],
        compiler_params=pltpu.CompilerParams(vmem_limit_bytes=2**20),
        name="write_out",
    )(*[pltpu.with_memory_space_constraint(o, pltpu.VMEM) for o in outs])
    output, input_grad, *grads = outs
    return output.reshape(CH * TB, DL), input_grad.reshape(CH * TB, DL), *grads


def solution(mesh):
    placed = (
        P("col", "row"),
        P("row", "col"),
        P("col"),
        P("col", "row"),
        P("row"),
        P("col", "row"),
    )
    return jax.shard_map(
        shards,
        mesh=mesh,
        in_specs=placed,
        out_specs=(
            P("col", "row"),
            P("col", "row"),
            P("row", "col"),
            P("col"),
            P("col", "row"),
            P("row"),
        ),
        check_vma=False,
    )
```

```python
import jax
import jax.numpy as jnp
from jax import lax
from jax.experimental import pallas as pl
from jax.experimental.pallas import tpu as pltpu
from jax.sharding import PartitionSpec as P

MESH = pl.DeviceIdType.MESH
BF16 = jnp.bfloat16
F32 = jnp.float32

CH = 5
TB = 16
ROWS = 256
HALF = ROWS // 2
DL = 768
FL = 1536
DH = DL // 2


SCHEDULE = (
    ("ag1", 0, 0), ("ag1", 0, 1), ("ag2", 0, 0), ("ag2", 0, 1), ("ag1", 1, 0), ("ag1", 1, 1), ("hid", 0, 0),
    ("hid", 0, 1), ("red1", 0, 0), ("ag2", 1, 0), ("ag2", 1, 1), ("ag1", 2, 0), ("ag1", 2, 1), ("red1", 0, 1),
    ("red2", 0, 0), ("hid", 1, 0), ("red2", 0, 1), ("hid", 1, 1), ("red1", 1, 0), ("ag2", 2, 0), ("ag2", 2, 1),
    ("ag1", 3, 0), ("ag1", 3, 1), ("gelu", 0, 0), ("red1", 1, 1), ("red2", 1, 0), ("gat2", 0, 0), ("hid", 2, 0),
    ("gat2", 0, 1), ("hid", 2, 1), ("red2", 1, 1), ("red1", 2, 0), ("ag2", 3, 0), ("ag2", 3, 1), ("ag1", 4, 0),
    ("ag1", 4, 1), ("red1", 2, 1), ("cg", 0, 0), ("cg", 0, 1), ("out", 0, 0), ("gelu", 1, 0), ("hid", 3, 0),
    ("out", 0, 1), ("red2", 2, 0), ("wt", 0, 0), ("hid", 3, 1), ("red2", 2, 1), ("red1", 3, 0), ("ag2", 4, 0),
    ("ag2", 4, 1), ("gat2", 1, 0), ("gat2", 1, 1), ("red1", 3, 1), ("rs2", 0, 0), ("gelu", 2, 0), ("red2", 3, 0),
    ("hid", 4, 0), ("cg", 1, 0), ("hid", 4, 1), ("red1", 4, 0), ("fin", 0, 0), ("cg", 1, 1), ("out", 1, 0),
    ("red1", 4, 1), ("red2", 3, 1), ("out", 1, 1), ("wt", 1, 0), ("gat2", 2, 0), ("gat2", 2, 1), ("red2", 4, 0),
    ("rs2", 1, 0), ("red2", 4, 1), ("gelu", 3, 0), ("cg", 2, 0), ("fin", 1, 0), ("cg", 2, 1), ("out", 2, 0),
    ("gelu", 4, 0), ("out", 2, 1), ("gat2", 3, 0), ("wt", 2, 0), ("gat2", 3, 1), ("gat2", 4, 0), ("gat2", 4, 1),
    ("cg", 3, 0), ("rs2", 2, 0), ("cg", 3, 1), ("out", 3, 0), ("cg", 4, 0), ("out", 3, 1), ("wt", 3, 0), ("cg", 4, 1),
    ("out", 4, 0), ("fin", 2, 0), ("out", 4, 1), ("wt", 4, 0), ("rs2", 3, 0), ("rs2", 4, 0), ("fin", 3, 0),
    ("fin", 4, 0),
)


def dot(a, b, dims):
    return lax.dot_general(a, b, ((dims[:1], dims[1:]), ((), ())), preferred_element_type=F32)


def body(
    x_hbm, g_hbm, w_in_hbm, w_out_hbm, b_in_hbm, b_out_hbm,
    out_o, out_i, w1g, out_b1, w2g, out_b2,
    xg, w_in, w_out, snd, crv, own, s, r1b, r2b, act, part, rab, sab, tab, b1g, b2g, b_in, b_out,
    load_sem, send_sem, ce_s, ag1_r, ag2_r, ce_r, y_r, gc_r, rs1_r, rs2_r,
):
    row, col = lax.axis_index("row"), lax.axis_index("col")
    y, core = row // 2, row % 2
    z, x = col // 4, col % 4
    abit, bbit = ((y + 1) // 2) % 2, y // 2
    ya, yb = y + 1 - 2 * (y % 2), 3 - y
    pair_a, pair_b = (ya * 2 + core, col), (yb * 2 + core, col)
    mate = (y * 2 + 1 - core, col)

    def zx(dz, dx):
        return (row, ((z + dz) % 4) * 4 + (x + dx) % 4)

    loads = [
        pltpu.make_async_copy(x_hbm, xg.at[:, 0, z, x], load_sem.at[0]),
        pltpu.make_async_copy(g_hbm, xg.at[:, 1, z, x], load_sem.at[1]),
        pltpu.make_async_copy(w_in_hbm, w_in, load_sem.at[2]),
        pltpu.make_async_copy(w_out_hbm, w_out, load_sem.at[3]),
        pltpu.make_async_copy(b_in_hbm, b_in, load_sem.at[4]),
        pltpu.make_async_copy(b_out_hbm, b_out, load_sem.at[5]),
    ]
    for cp in loads:
        cp.start()

    barrier = pltpu.get_barrier_semaphore()
    peers = [pair_a, pair_b, mate] + [zx(0, d) for d in (1, 2, 3)] + [zx(d, 0) for d in (1, 2, 3)]
    for p in peers:
        pl.semaphore_signal(barrier, inc=1, device_id=p, device_id_type=MESH)
    pl.semaphore_wait(barrier, len(peers))
    loads[0].wait()
    loads[1].wait()

    def rcopy(src, dst, ss, rs, dev):
        return lambda: pltpu.make_async_remote_copy(
            src_ref=src, dst_ref=dst, send_sem=ss, recv_sem=rs, device_id=dev, device_id_type=MESH
        ).start()

    lo, hi = pl.ds(0, DH), pl.ds(DH, DH)

    def ag1(c, t):
        rs = ag1_r.at[c, t]
        res = []
        for d in (1, 2, 3):
            ref = xg.at[c, t, z, x, :, lo]
            res.append(rcopy(ref, ref, send_sem.at[0], rs, zx(0, d)))
            ref = xg.at[c, t, z, x, :, hi]
            res.append(rcopy(ref, ref, send_sem.at[0], rs, zx(d, 0)))
        return res, xg.at[c, t, 0, 0:3], rs

    def ag2(c, t):
        rs = ag2_r.at[c, t]
        res = []
        for d in (1, 2, 3):
            ref = xg.at[c, t, z, :, :, lo]
            res.append(rcopy(ref, ref, send_sem.at[1], rs, zx(d, 0)))
            ref = xg.at[c, t, :, x, :, hi]
            res.append(rcopy(ref, ref, send_sem.at[1], rs, zx(0, d)))
        return res, xg.at[c, t, 0:3], rs

    def core_swap(c, t):
        rs = ce_r.at[c, t]
        return [rcopy(snd.at[t], crv.at[c, t], ce_s.at[t], rs, mate)], crv.at[c, t], rs

    def rows(start, n):
        return pl.ds(pl.multiple_of(start, TB), n)

    a_keep, a_send = abit * 32, (1 - abit) * 32
    b_keep, b_send = 64 + bbit * 32, 64 + (1 - bbit) * 32
    a_own, a_send2 = a_keep + bbit * 16, a_keep + (1 - bbit) * 16
    b_own, b_send2 = b_keep + abit * 16, b_keep + (1 - abit) * 16

    def y_red1(c, t):
        ss, rs = send_sem.at[2], y_r.at[c, t, 0]
        return [
            rcopy(s.at[c, t, rows(a_send, 32)], r1b.at[c, t, 0], ss, rs, pair_a),
            rcopy(s.at[c, t, rows(b_send, 32)], r1b.at[c, t, 1], ss, rs, pair_b),
        ], r1b.at[c, t], rs

    def y_red2(c, t):
        ss, rs = send_sem.at[3], y_r.at[c, t, 1]
        return [
            rcopy(s.at[c, t, rows(a_send2, 16)], r2b.at[c, t, 0], ss, rs, pair_b),
            rcopy(s.at[c, t, rows(b_send2, 16)], r2b.at[c, t, 1], ss, rs, pair_a),
        ], r2b.at[c, t], rs

    def y_gat1(c, t):
        ss, rs = send_sem.at[4], y_r.at[c, t, 2]
        ref_a = act.at[c, t, rows(core * HALF + a_own, 16)]
        ref_b = act.at[c, t, rows(core * HALF + b_own, 16)]
        return [rcopy(ref_a, ref_a, ss, rs, pair_b), rcopy(ref_b, ref_b, ss, rs, pair_a)], act.at[c, t, 0:32], rs

    def y_gat2(c, t):
        ss, rs = send_sem.at[5], y_r.at[c, t, 3]
        ref_a = act.at[c, t, rows(core * HALF + a_keep, 32)]
        ref_b = act.at[c, t, rows(core * HALF + b_keep, 32)]
        return [rcopy(ref_a, ref_a, ss, rs, pair_a), rcopy(ref_b, ref_b, ss, rs, pair_b)], act.at[c, t, 0:64], rs

    def core_gat(c, t):
        rs = gc_r.at[c, t]
        ref = act.at[c, t, rows(core * HALF, HALF)]
        return [rcopy(ref, ref, send_sem.at[6], rs, mate)], act.at[c, t, 0:HALF], rs

    def rs1(c, t):
        ss, rs = send_sem.at[7], rs1_r.at[c, t]
        res = []
        for d in (1, 2, 3):
            src = part.at[c, t, :, (x + d) % 4, :, lo]
            res.append(rcopy(src, rab.at[c, t, 0, d - 1], ss, rs, zx(0, d)))
            src = part.at[c, t, (z + d) % 4, :, :, hi]
            res.append(rcopy(src, rab.at[c, t, 1, d - 1], ss, rs, zx(d, 0)))
        return res, rab.at[c, t], rs

    def rs2(c):
        ss, rs = send_sem.at[8], rs2_r.at[c]
        res = []
        for d in (1, 2, 3):
            src = sab.at[c, 0, :, (z + d) % 4]
            res.append(rcopy(src, tab.at[c, 0, d - 1], ss, rs, zx(d, 0)))
            src = sab.at[c, 1, :, (x + d) % 4]
            res.append(rcopy(src, tab.at[c, 1, d - 1], ss, rs, zx(0, d)))
        return res, tab.at[c], rs

    def start(stage):
        for send in stage[0]:
            send()

    def wait_bytes(size, sem):
        pltpu.make_async_copy(size, size, sem).wait()

    def wait(stage):
        wait_bytes(*stage[1:])

    def half_of(c, t, which):
        return xg[c, t, pl.ds(2 * which, 2)].reshape(HALF, DL)

    def chunk_of(c, t):
        return xg[c, t].reshape(ROWS, DL)

    def ag1_stage(c, t):
        start(ag1(c, t))

    def ag2_stage(c, t):
        wait(ag1(c, t))
        start(ag2(c, t))

    def hidden_stage(c, t):
        if c == 0:
            loads[2 + t].wait()
            loads[4 + t].wait()
        wait(ag2(c, t))
        lhs = jnp.concatenate([half_of(c, t, 1 - core), half_of(c, t, core)], axis=0)
        for n in range(0, FL, 512):
            if t == 0:
                r = dot(lhs, w_in[:, n:n + 512], (1, 0))
            else:
                r = dot(lhs, w_out[n:n + 512, :], (1, 1))
            snd[t, :, n:n + 512] = r[:HALF].astype(BF16)
            own[t, :, n:n + 512] = r[HALF:]
        start(core_swap(c, t))

    def red1_stage(c, t):
        wait(core_swap(c, t))
        wait_bytes(snd.at[t], ce_s.at[t])
        s[c, t] = (own[t] + crv[c, t].astype(F32)).astype(BF16)
        start(y_red1(c, t))

    def red2_stage(c, t):
        wait(y_red1(c, t))
        for k, keep in ((0, a_keep), (1, b_keep)):
            here = s.at[c, t, rows(keep, 32)]
            here[...] = (here[...].astype(F32) + r1b[c, t, k].astype(F32)).astype(BF16)
        start(y_red2(c, t))

    def gelu_stage(c, _):
        wait(y_red2(c, 0))
        wait(y_red2(c, 1))
        for k, mine in ((0, a_own), (1, b_own)):
            total = s[c, :, rows(mine, 16)].astype(F32) + r2b[c, :, k].astype(F32)
            hidden = total[0] + b_in[...][None]
            half = 0.5 * (1.0 + lax.erf(hidden * 0.7071067811865476))
            slope = half + hidden * jnp.exp(-0.5 * hidden * hidden) * 0.3989422804014327
            at = rows(core * HALF + mine, 16)
            act[c, 0, at] = (hidden * half).astype(BF16)
            act[c, 1, at] = (total[1] * slope).astype(BF16)
        start(y_gat1(c, 0))
        start(y_gat1(c, 1))

    def gat2_stage(c, t):
        wait(y_gat1(c, t))
        start(y_gat2(c, t))

    def core_gat_stage(c, t):
        wait(y_gat2(c, t))
        start(core_gat(c, t))

    def out_stage(c, t):
        wait(core_gat(c, t))
        for n in range(0, DL, 256):
            if t == 0:
                r = dot(act[c, 0], w_out[:, n:n + 256], (1, 0))
            else:
                r = dot(act[c, 1], w_in[n:n + 256, :], (1, 1))
            part[c, t, :, :, :, n:n + 256] = r.astype(BF16).reshape(4, 4, TB, 256)
        start(rs1(c, t))

    def rs2_stage(c, _):
        for t in (0, 1):
            wait(rs1(c, t))
            total = part[c, t, :, x, :, lo].astype(F32)
            for d in range(3):
                total += rab[c, t, 0, d].astype(F32)
            sab[c, 0, t] = total.astype(BF16)
            total = part[c, t, z, :, :, hi].astype(F32)
            for d in range(3):
                total += rab[c, t, 1, d].astype(F32)
            sab[c, 1, t] = total.astype(BF16)
        start(rs2(c))

    def final_stage(c, _):
        wait(rs2(c))
        for k, me, cols in ((0, z, lo), (1, x, hi)):
            total = sab[c, k, :, me].astype(F32)
            for d in range(3):
                total += tab[c, k, d].astype(F32)
            out_o[c, :, cols] = (total[0] + b_out[cols][None]).astype(BF16)
            out_i[c, :, cols] = total[1].astype(BF16)

    def weight_stage(c, _):
        def add(ref, at, value):
            ref[at] = value if c == 0 else ref[at] + value

        g_k = chunk_of(c, 1)
        for n in range(0, FL, 512):
            add(w2g, (slice(n, n + 512), slice(None)), dot(act[c, 0, :, n:n + 512], g_k, (0, 0)))
        x_k = chunk_of(c, 0)
        for n in range(0, FL, 512):
            add(w1g, (slice(None), slice(n, n + 512)), dot(x_k, act[c, 1, :, n:n + 512], (0, 0)))
        add(b1g, ..., jnp.sum(act[c, 1].astype(F32), axis=0, keepdims=True))
        add(b2g, ..., jnp.sum(g_k.astype(F32), axis=0, keepdims=True))

    stages = dict(
        ag1=ag1_stage, ag2=ag2_stage, hid=hidden_stage, red1=red1_stage, red2=red2_stage, gelu=gelu_stage,
        gat2=gat2_stage, cg=core_gat_stage, out=out_stage, rs2=rs2_stage, fin=final_stage, wt=weight_stage,
    )
    for name, c, t in SCHEDULE:
        stages[name](c, t)

    sent = (
        xg.at[:, :, 0, 0:3], xg.at[:, :, 0:3], r1b, r2b, act.at[:, :, 0:32], act.at[:, :, 0:64],
        act.at[:, :, 0:HALF], rab, tab,
    )
    for k, size in enumerate(sent):
        wait_bytes(size, send_sem.at[k])
    out_b1[...] = jnp.sum(b1g[...], axis=0)
    out_b2[...] = jnp.sum(b2g[...], axis=0)


def write_out(*refs):
    sems = refs[-1]
    copies = [pltpu.make_async_copy(refs[k], refs[k + 6], sems.at[k]) for k in range(6)]
    for cp in copies:
        cp.start()
    for cp in copies:
        cp.wait()


def shards(inputs, w_in, b_in, w_out, b_out, out_grad):
    any_spec = pl.BlockSpec(memory_space=pl.ANY)
    vmem_spec = pl.BlockSpec(memory_space=pltpu.VMEM)
    dma = pltpu.SemaphoreType.DMA
    outs = pl.pallas_call(
        body,
        out_shape=[
            pltpu.VMEM((CH, TB, DL), BF16),
            pltpu.VMEM((CH, TB, DL), BF16),
            pltpu.VMEM((DL, FL), F32),
            pltpu.VMEM((FL,), F32),
            pltpu.VMEM((FL, DL), F32),
            pltpu.VMEM((DL,), F32),
        ],
        in_specs=[any_spec] * 6,
        out_specs=[vmem_spec] * 6,
        scratch_shapes=[
            pltpu.VMEM((CH, 2, 4, 4, TB, DL), BF16),
            pltpu.VMEM((DL, FL), BF16),
            pltpu.VMEM((FL, DL), BF16),
            pltpu.VMEM((2, HALF, FL), BF16),
            pltpu.VMEM((CH, 2, HALF, FL), BF16),
            pltpu.VMEM((2, HALF, FL), F32),
            pltpu.VMEM((CH, 2, HALF, FL), BF16),
            pltpu.VMEM((CH, 2, 2, 32, FL), BF16),
            pltpu.VMEM((CH, 2, 2, 16, FL), BF16),
            pltpu.VMEM((CH, 2, ROWS, FL), BF16),
            pltpu.VMEM((CH, 2, 4, 4, TB, DL), BF16),
            pltpu.VMEM((CH, 2, 2, 3, 4, TB, DH), BF16),
            pltpu.VMEM((CH, 2, 2, 4, TB, DH), BF16),
            pltpu.VMEM((CH, 2, 3, 2, TB, DH), BF16),
            pltpu.VMEM((1, FL), F32),
            pltpu.VMEM((1, DL), F32),
            pltpu.VMEM((FL,), F32),
            pltpu.VMEM((DL,), F32),
            dma((6,)),
            dma((9,)), dma((2,)),
            dma((CH, 2)), dma((CH, 2)), dma((CH, 2)), dma((CH, 2, 4)), dma((CH, 2)), dma((CH, 2)), dma((CH,)),
        ],
        compiler_params=pltpu.CompilerParams(
            collective_id=0, has_side_effects=True, vmem_limit_bytes=48 * 2**20
        ),
        cost_estimate=pl.CostEstimate(flops=18 * 10**9, bytes_accessed=15 * 10**6, transcendentals=10**6),
        name="mlp",
    )(
        inputs.reshape(CH, TB, DL), out_grad.reshape(CH, TB, DL), w_in, w_out,
        b_in, b_out,
    )
    outs = pl.pallas_call(
        write_out,
        out_shape=[jax.ShapeDtypeStruct(o.shape, o.dtype) for o in outs],
        in_specs=[vmem_spec] * 6,
        out_specs=[any_spec] * 6,
        scratch_shapes=[dma((6,))],
        compiler_params=pltpu.CompilerParams(vmem_limit_bytes=2**20),
        name="write_out",
    )(*[pltpu.with_memory_space_constraint(o, pltpu.VMEM) for o in outs])
    output, input_grad, *grads = outs
    return output.reshape(CH * TB, DL), input_grad.reshape(CH * TB, DL), *grads


def solution(mesh):
    placed = (
        P("col", "row"),
        P("row", "col"),
        P("col"),
        P("col", "row"),
        P("row"),
        P("col", "row"),
    )
    return jax.shard_map(
        shards,
        mesh=mesh,
        in_specs=placed,
        out_specs=(
            P("col", "row"),
            P("col", "row"),
            P("row", "col"),
            P("col"),
            P("col", "row"),
            P("row"),
        ),
        check_vma=False,
    )
```

```python
import jax
import jax.numpy as jnp
from jax import lax
from jax.experimental import pallas as pl
from jax.experimental.pallas import tpu as pltpu
from jax.sharding import PartitionSpec as P

MESH = pl.DeviceIdType.MESH
BF16 = jnp.bfloat16
F32 = jnp.float32

CH = 5
TB = 16
ROWS = 256
HALF = ROWS // 2
DL = 768
FL = 1536
DH = DL // 2


SCHEDULE = (
    ("ag1", 0, 0), ("ag1", 1, 0), ("ag1", 1, 1), ("ag1", 0, 1), ("ag2", 0, 0), ("ag2", 0, 1), ("ag2", 1, 0),
    ("hid", 0, 0), ("ag1", 2, 0), ("hid", 0, 1), ("red1", 0, 0), ("ag1", 2, 1), ("ag2", 1, 1), ("red1", 0, 1),
    ("hid", 1, 0), ("red2", 0, 0), ("ag2", 2, 0), ("ag1", 3, 0), ("ag2", 2, 1), ("red1", 1, 0), ("hid", 1, 1),
    ("red2", 0, 1), ("red1", 1, 1), ("hid", 2, 0), ("ag1", 3, 1), ("ag1", 4, 0), ("gelu", 0, 2), ("hid", 2, 1),
    ("ag2", 3, 0), ("ag1", 4, 1), ("red2", 1, 2), ("red1", 2, 2), ("gat2", 0, 2), ("hid", 3, 0), ("gelu", 1, 2),
    ("ag2", 3, 1), ("hid", 3, 1), ("ag2", 4, 0), ("red2", 2, 2), ("cg", 0, 2), ("red1", 3, 2), ("ag2", 4, 1),
    ("hid", 4, 0), ("gelu", 2, 2), ("gat2", 1, 2), ("hid", 4, 1), ("red1", 4, 2), ("cg", 1, 2), ("red2", 3, 2),
    ("gat2", 2, 2), ("out", 0, 0), ("out", 1, 0), ("gelu", 3, 2), ("out", 0, 1), ("red2", 4, 2), ("wt", 0, 2),
    ("cg", 2, 2), ("out", 1, 1), ("rs2", 0, 2), ("gat2", 3, 0), ("out", 2, 0), ("gelu", 4, 2), ("gat2", 3, 1),
    ("wt", 1, 2), ("out", 2, 1), ("cg", 3, 0), ("rs2", 1, 2), ("gat2", 4, 0), ("out", 3, 0), ("cg", 3, 1),
    ("gat2", 4, 1), ("rs2", 2, 2), ("out", 3, 1), ("cg", 4, 0), ("fin", 0, 2), ("outa", 4, 0), ("wt", 2, 2),
    ("outb", 4, 0), ("fin", 1, 2), ("cg", 4, 1), ("outa", 4, 1), ("fin", 2, 2), ("outb", 4, 1), ("rs2", 3, 2),
    ("wt", 3, 2), ("rs2", 4, 0), ("rs2", 4, 1), ("wt", 4, 2), ("fin", 3, 2), ("fin", 4, 0), ("fin", 4, 1),
)


def dot(a, b, dims):
    return lax.dot_general(a, b, ((dims[:1], dims[1:]), ((), ())), preferred_element_type=F32)


def body(
    x_hbm, g_hbm, w_in_hbm, w_out_hbm, b_in_hbm, b_out_hbm,
    out_o, out_i, w1g, out_b1, w2g, out_b2,
    xg, w_in, w_out, snd, crv, own, s, r1b, r2b, act, part, rab, sab, tab, b1g, b2g, b_in, b_out,
    load_sem, send_sem, ce_s, ag1_r, ag2_r, ce_r, y_r, gc_r, rs1_r, rs2_r,
):
    row, col = lax.axis_index("row"), lax.axis_index("col")
    y, core = row // 2, row % 2
    z, x = col // 4, col % 4
    abit, bbit = ((y + 1) // 2) % 2, y // 2
    ya, yb = y + 1 - 2 * (y % 2), 3 - y
    pair_a, pair_b = (ya * 2 + core, col), (yb * 2 + core, col)
    mate = (y * 2 + 1 - core, col)

    def zx(dz, dx):
        return (row, ((z + dz) % 4) * 4 + (x + dx) % 4)

    loads = [
        pltpu.make_async_copy(x_hbm, xg.at[:, 0, z, x], load_sem.at[0]),
        pltpu.make_async_copy(g_hbm, xg.at[:, 1, z, x], load_sem.at[1]),
        pltpu.make_async_copy(w_in_hbm, w_in, load_sem.at[2]),
        pltpu.make_async_copy(w_out_hbm, w_out, load_sem.at[3]),
        pltpu.make_async_copy(b_in_hbm, b_in, load_sem.at[4]),
        pltpu.make_async_copy(b_out_hbm, b_out, load_sem.at[5]),
    ]
    for cp in loads:
        cp.start()

    barrier = pltpu.get_barrier_semaphore()
    peers = [pair_a, pair_b, mate] + [zx(0, d) for d in (1, 2, 3)] + [zx(d, 0) for d in (1, 2, 3)]
    for p in peers:
        pl.semaphore_signal(barrier, inc=1, device_id=p, device_id_type=MESH)
    pl.semaphore_wait(barrier, len(peers))
    loads[0].wait()
    loads[1].wait()

    def rcopy(src, dst, ss, rs, dev):
        return lambda: pltpu.make_async_remote_copy(
            src_ref=src, dst_ref=dst, send_sem=ss, recv_sem=rs, device_id=dev, device_id_type=MESH
        ).start()

    lo, hi = pl.ds(0, DH), pl.ds(DH, DH)

    def ag1(c, t):
        rs = ag1_r.at[c, t]
        res = []
        for d in (1, 2, 3):
            ref = xg.at[c, t, z, x, :, lo]
            res.append(rcopy(ref, ref, send_sem.at[0], rs, zx(0, d)))
            ref = xg.at[c, t, z, x, :, hi]
            res.append(rcopy(ref, ref, send_sem.at[0], rs, zx(d, 0)))
        return res, xg.at[c, t, 0, 0:3], rs

    def ag2(c, t):
        rs = ag2_r.at[c, t]
        res = []
        for d in (1, 2, 3):
            ref = xg.at[c, t, z, :, :, lo]
            res.append(rcopy(ref, ref, send_sem.at[1], rs, zx(d, 0)))
            ref = xg.at[c, t, :, x, :, hi]
            res.append(rcopy(ref, ref, send_sem.at[1], rs, zx(0, d)))
        return res, xg.at[c, t, 0:3], rs

    def core_swap(c, t):
        rs = ce_r.at[c, t]
        return [rcopy(snd.at[t], crv.at[c, t], ce_s.at[t], rs, mate)], crv.at[c, t], rs

    def rows(start, n):
        return pl.ds(pl.multiple_of(start, TB), n)

    a_keep, a_send = abit * 32, (1 - abit) * 32
    b_keep, b_send = 64 + bbit * 32, 64 + (1 - bbit) * 32
    a_own, a_send2 = a_keep + bbit * 16, a_keep + (1 - bbit) * 16
    b_own, b_send2 = b_keep + abit * 16, b_keep + (1 - abit) * 16

    def pick(t):
        return slice(None) if t == 2 else t

    def parts(t):
        return (0, 1) if t == 2 else (t,)

    def sent_as(name, c, t):
        return (2,) if (name, c, 2) in SCHEDULE else parts(t)

    def y_red1(c, t):
        ss, rs = send_sem.at[2], y_r.at[c, t % 2, 0]
        t = pick(t)
        return [
            rcopy(s.at[c, t, rows(a_send, 32)], r1b.at[c, t, 0], ss, rs, pair_a),
            rcopy(s.at[c, t, rows(b_send, 32)], r1b.at[c, t, 1], ss, rs, pair_b),
        ], r1b.at[c, t], rs

    def y_red2(c, t):
        ss, rs = send_sem.at[3], y_r.at[c, t % 2, 1]
        t = pick(t)
        return [
            rcopy(s.at[c, t, rows(a_send2, 16)], r2b.at[c, t, 0], ss, rs, pair_b),
            rcopy(s.at[c, t, rows(b_send2, 16)], r2b.at[c, t, 1], ss, rs, pair_a),
        ], r2b.at[c, t], rs

    def y_gat1(c):
        ss, rs = send_sem.at[4], y_r.at[c, 0, 2]
        ref_a = act.at[c, :, rows(core * HALF + a_own, 16)]
        ref_b = act.at[c, :, rows(core * HALF + b_own, 16)]
        return [rcopy(ref_a, ref_a, ss, rs, pair_b), rcopy(ref_b, ref_b, ss, rs, pair_a)], act.at[c, :, 0:32], rs

    def y_gat2(c, t):
        ss, rs = send_sem.at[5], y_r.at[c, t % 2, 3]
        t = pick(t)
        ref_a = act.at[c, t, rows(core * HALF + a_keep, 32)]
        ref_b = act.at[c, t, rows(core * HALF + b_keep, 32)]
        return [rcopy(ref_a, ref_a, ss, rs, pair_a), rcopy(ref_b, ref_b, ss, rs, pair_b)], act.at[c, t, 0:64], rs

    def core_gat(c, t):
        rs = gc_r.at[c, t % 2]
        t = pick(t)
        ref = act.at[c, t, rows(core * HALF, HALF)]
        return [rcopy(ref, ref, send_sem.at[6], rs, mate)], act.at[c, t, 0:HALF], rs

    def rs1(c, t):
        ss, rs = send_sem.at[7], rs1_r.at[c, t]
        res = []
        for d in (1, 2, 3):
            src = part.at[c, t, :, (x + d) % 4, :, lo]
            res.append(rcopy(src, rab.at[c, t, 0, d - 1], ss, rs, zx(0, d)))
            src = part.at[c, t, (z + d) % 4, :, :, hi]
            res.append(rcopy(src, rab.at[c, t, 1, d - 1], ss, rs, zx(d, 0)))
        return res, rab.at[c, t], rs

    def rs1_half(c, t, which):
        ss, rs = send_sem.at[7], rs1_r.at[c, t]
        z_two = pl.ds(2 * which, 2)
        for d in (1, 2, 3):
            src = part.at[c, t, z_two, (x + d) % 4, :, lo]
            rcopy(src, rab.at[c, t, 0, d - 1, z_two], ss, rs, zx(0, d))()
            src = part.at[c, t, (z + d) % 4, :, :, hi]
            pl.when((z + d) % 4 // 2 == which)(rcopy(src, rab.at[c, t, 1, d - 1], ss, rs, zx(d, 0)))

    def rs2(c, t):
        ss, rs = send_sem.at[8], rs2_r.at[c, t % 2]
        t = pick(t)
        res = []
        for d in (1, 2, 3):
            src = sab.at[c, 0, t, (z + d) % 4]
            res.append(rcopy(src, tab.at[c, 0, d - 1, t], ss, rs, zx(d, 0)))
            src = sab.at[c, 1, t, (x + d) % 4]
            res.append(rcopy(src, tab.at[c, 1, d - 1, t], ss, rs, zx(0, d)))
        return res, tab.at[c, :, :, t], rs

    def start(stage):
        for send in stage[0]:
            send()

    def wait_bytes(size, sem):
        pltpu.make_async_copy(size, size, sem).wait()

    def wait(stage):
        wait_bytes(*stage[1:])

    def half_of(c, t, which):
        return xg[c, t, pl.ds(2 * which, 2)].reshape(HALF, DL)

    def chunk_of(c, t):
        return xg[c, t].reshape(ROWS, DL)

    def ag1_stage(c, t):
        start(ag1(c, t))

    def ag2_stage(c, t):
        wait(ag1(c, t))
        start(ag2(c, t))

    def hidden_stage(c, t):
        if c == 0:
            loads[2 + t].wait()
            loads[4 + t].wait()
        wait(ag2(c, t))
        lhs = jnp.concatenate([half_of(c, t, 1 - core), half_of(c, t, core)], axis=0)
        for n in range(0, FL, 512):
            if t == 0:
                r = dot(lhs, w_in[:, n:n + 512], (1, 0))
            else:
                r = dot(lhs, w_out[n:n + 512, :], (1, 1))
            snd[t, :, n:n + 512] = r[:HALF].astype(BF16)
            own[t, :, n:n + 512] = r[HALF:]
        start(core_swap(c, t))

    def red1_stage(c, t):
        for p in parts(t):
            wait(core_swap(c, p))
            wait_bytes(snd.at[p], ce_s.at[p])
            s[c, p] = (own[p] + crv[c, p].astype(F32)).astype(BF16)
        start(y_red1(c, t))

    def red2_stage(c, t):
        for p in sent_as("red1", c, t):
            wait(y_red1(c, p))
        for p in parts(t):
            for k, keep in ((0, a_keep), (1, b_keep)):
                here = s.at[c, p, rows(keep, 32)]
                here[...] = (here[...].astype(F32) + r1b[c, p, k].astype(F32)).astype(BF16)
        start(y_red2(c, t))

    def gelu_stage(c, _):
        for p in sent_as("red2", c, 2):
            wait(y_red2(c, p))
        for k, mine in ((0, a_own), (1, b_own)):
            total = s[c, :, rows(mine, 16)].astype(F32) + r2b[c, :, k].astype(F32)
            hidden = total[0] + b_in[...][None]
            half = 0.5 * (1.0 + lax.erf(hidden * 0.7071067811865476))
            slope = half + hidden * jnp.exp(-0.5 * hidden * hidden) * 0.3989422804014327
            at = rows(core * HALF + mine, 16)
            act[c, 0, at] = (hidden * half).astype(BF16)
            act[c, 1, at] = (total[1] * slope).astype(BF16)
        start(y_gat1(c))

    def gat2_stage(c, t):
        if t != 1:
            wait(y_gat1(c))
        start(y_gat2(c, t))

    def core_gat_stage(c, t):
        wait(y_gat2(c, t))
        start(core_gat(c, t))

    def out_stage(c, t):
        if t in sent_as("cg", c, t):
            wait(core_gat(c, t))
        elif t == 0:
            wait(core_gat(c, 2))
        for n in range(0, DL, 256):
            if t == 0:
                r = dot(act[c, 0], w_out[:, n:n + 256], (1, 0))
            else:
                r = dot(act[c, 1], w_in[n:n + 256, :], (1, 1))
            part[c, t, :, :, :, n:n + 256] = r.astype(BF16).reshape(4, 4, TB, 256)
        start(rs1(c, t))

    def out_half(c, t, which):
        at = rows(which * HALF, HALF)
        for n in range(0, DL, 256):
            if t == 0:
                r = dot(act[c, 0, at], w_out[:, n:n + 256], (1, 0))
            else:
                r = dot(act[c, 1, at], w_in[n:n + 256, :], (1, 1))
            part[c, t, pl.ds(2 * which, 2), :, :, n:n + 256] = r.astype(BF16).reshape(2, 4, TB, 256)
        rs1_half(c, t, which)

    def out_own_stage(c, t):
        out_half(c, t, core)

    def out_other_stage(c, t):
        if t in sent_as("cg", c, t):
            wait(core_gat(c, t))
        elif t == 0:
            wait(core_gat(c, 2))
        out_half(c, t, 1 - core)

    def rs2_stage(c, t):
        for p in parts(t):
            wait(rs1(c, p))
            total = part[c, p, :, x, :, lo].astype(F32)
            for d in range(3):
                total += rab[c, p, 0, d].astype(F32)
            sab[c, 0, p] = total.astype(BF16)
            total = part[c, p, z, :, :, hi].astype(F32)
            for d in range(3):
                total += rab[c, p, 1, d].astype(F32)
            sab[c, 1, p] = total.astype(BF16)
        start(rs2(c, t))

    def final_stage(c, t):
        wait(rs2(c, t))
        for k, me, cols in ((0, z, lo), (1, x, hi)):
            for p in parts(t):
                total = sab[c, k, p, me].astype(F32)
                for d in range(3):
                    total += tab[c, k, d, p].astype(F32)
                if p == 0:
                    out_o[c, :, cols] = (total + b_out[cols][None]).astype(BF16)
                else:
                    out_i[c, :, cols] = total.astype(BF16)

    def weight_stage(c, _):
        def add(ref, at, value):
            ref[at] = value if c == 0 else ref[at] + value

        g_k = chunk_of(c, 1)
        for n in range(0, FL, 512):
            add(w2g, (slice(n, n + 512), slice(None)), dot(act[c, 0, :, n:n + 512], g_k, (0, 0)))
        x_k = chunk_of(c, 0)
        for n in range(0, FL, 512):
            add(w1g, (slice(None), slice(n, n + 512)), dot(x_k, act[c, 1, :, n:n + 512], (0, 0)))
        add(b1g, ..., jnp.sum(act[c, 1].astype(F32), axis=0, keepdims=True))
        add(b2g, ..., jnp.sum(g_k.astype(F32), axis=0, keepdims=True))

    stages = dict(
        ag1=ag1_stage, ag2=ag2_stage, hid=hidden_stage, red1=red1_stage, red2=red2_stage, gelu=gelu_stage,
        gat2=gat2_stage, cg=core_gat_stage, out=out_stage,
        outa=out_own_stage, outb=out_other_stage, rs2=rs2_stage, fin=final_stage, wt=weight_stage,
    )
    for name, c, t in SCHEDULE:
        stages[name](c, t)

    sent = (
        xg.at[:, :, 0, 0:3], xg.at[:, :, 0:3], r1b, r2b, act.at[:, :, 0:32], act.at[:, :, 0:64],
        act.at[:, :, 0:HALF], rab, tab,
    )
    for k, size in enumerate(sent):
        wait_bytes(size, send_sem.at[k])
    out_b1[...] = jnp.sum(b1g[...], axis=0)
    out_b2[...] = jnp.sum(b2g[...], axis=0)


def write_out(*refs):
    sems = refs[-1]
    copies = [pltpu.make_async_copy(refs[k], refs[k + 6], sems.at[k]) for k in range(6)]
    for cp in copies:
        cp.start()
    for cp in copies:
        cp.wait()


def shards(inputs, w_in, b_in, w_out, b_out, out_grad):
    any_spec = pl.BlockSpec(memory_space=pl.ANY)
    vmem_spec = pl.BlockSpec(memory_space=pltpu.VMEM)
    dma = pltpu.SemaphoreType.DMA
    outs = pl.pallas_call(
        body,
        out_shape=[
            pltpu.VMEM((CH, TB, DL), BF16),
            pltpu.VMEM((CH, TB, DL), BF16),
            pltpu.VMEM((DL, FL), F32),
            pltpu.VMEM((FL,), F32),
            pltpu.VMEM((FL, DL), F32),
            pltpu.VMEM((DL,), F32),
        ],
        in_specs=[any_spec] * 6,
        out_specs=[vmem_spec] * 6,
        scratch_shapes=[
            pltpu.VMEM((CH, 2, 4, 4, TB, DL), BF16),
            pltpu.VMEM((DL, FL), BF16),
            pltpu.VMEM((FL, DL), BF16),
            pltpu.VMEM((2, HALF, FL), BF16),
            pltpu.VMEM((CH, 2, HALF, FL), BF16),
            pltpu.VMEM((2, HALF, FL), F32),
            pltpu.VMEM((CH, 2, HALF, FL), BF16),
            pltpu.VMEM((CH, 2, 2, 32, FL), BF16),
            pltpu.VMEM((CH, 2, 2, 16, FL), BF16),
            pltpu.VMEM((CH, 2, ROWS, FL), BF16),
            pltpu.VMEM((CH, 2, 4, 4, TB, DL), BF16),
            pltpu.VMEM((CH, 2, 2, 3, 4, TB, DH), BF16),
            pltpu.VMEM((CH, 2, 2, 4, TB, DH), BF16),
            pltpu.VMEM((CH, 2, 3, 2, TB, DH), BF16),
            pltpu.VMEM((1, FL), F32),
            pltpu.VMEM((1, DL), F32),
            pltpu.VMEM((FL,), F32),
            pltpu.VMEM((DL,), F32),
            dma((6,)),
            dma((9,)), dma((2,)),
            dma((CH, 2)), dma((CH, 2)), dma((CH, 2)), dma((CH, 2, 4)), dma((CH, 2)), dma((CH, 2)), dma((CH, 2)),
        ],
        compiler_params=pltpu.CompilerParams(
            collective_id=0, has_side_effects=True, vmem_limit_bytes=48 * 2**20
        ),
        cost_estimate=pl.CostEstimate(flops=18 * 10**9, bytes_accessed=15 * 10**6, transcendentals=10**6),
        name="mlp",
    )(
        inputs.reshape(CH, TB, DL), out_grad.reshape(CH, TB, DL), w_in, w_out,
        b_in, b_out,
    )
    outs = pl.pallas_call(
        write_out,
        out_shape=[jax.ShapeDtypeStruct(o.shape, o.dtype) for o in outs],
        in_specs=[vmem_spec] * 6,
        out_specs=[any_spec] * 6,
        scratch_shapes=[dma((6,))],
        compiler_params=pltpu.CompilerParams(vmem_limit_bytes=2**20),
        name="write_out",
    )(*[pltpu.with_memory_space_constraint(o, pltpu.VMEM) for o in outs])
    output, input_grad, *grads = outs
    return output.reshape(CH * TB, DL), input_grad.reshape(CH * TB, DL), *grads


def solution(mesh):
    placed = (
        P("col", "row"),
        P("row", "col"),
        P("col"),
        P("col", "row"),
        P("row"),
        P("col", "row"),
    )
    return jax.shard_map(
        shards,
        mesh=mesh,
        in_specs=placed,
        out_specs=(
            P("col", "row"),
            P("col", "row"),
            P("row", "col"),
            P("col"),
            P("col", "row"),
            P("row"),
        ),
        check_vma=False,
    )
```

```python
import jax
import jax.numpy as jnp
from jax import lax
from jax.experimental import pallas as pl
from jax.experimental.pallas import tpu as pltpu
from jax.sharding import PartitionSpec as P

MESH = pl.DeviceIdType.MESH
BF16 = jnp.bfloat16
F32 = jnp.float32

CH = 5
TB = 16
ROWS = 256
HALF = ROWS // 2
DL = 768
FL = 1536
DH = DL // 2


SCHEDULE = (
    ("ag1", 0, 0), ("ag1", 1, 0), ("ag1", 1, 1), ("ag1", 0, 1), ("ag2", 0, 0), ("ag2", 0, 1), ("ag2", 1, 0),
    ("hid", 0, 0), ("ag1", 2, 0), ("hid", 0, 1), ("red1", 0, 0), ("ag1", 2, 1), ("ag2", 1, 1), ("red1", 0, 1),
    ("hid", 1, 0), ("red2", 0, 0), ("ag2", 2, 0), ("ag1", 3, 0), ("ag2", 2, 1), ("red1", 1, 0), ("hid", 1, 1),
    ("red2", 0, 1), ("red1", 1, 1), ("hid", 2, 0), ("ag1", 3, 1), ("ag1", 4, 0), ("gelu", 0, 2), ("hid", 2, 1),
    ("ag2", 3, 0), ("ag1", 4, 1), ("red2", 1, 2), ("red1", 2, 2), ("gat2", 0, 2), ("hid", 3, 0), ("gelu", 1, 2),
    ("ag2", 3, 1), ("hid", 3, 1), ("ag2", 4, 0), ("red2", 2, 2), ("cg", 0, 2), ("red1", 3, 2), ("ag2", 4, 1),
    ("hid", 4, 0), ("gelu", 2, 2), ("gat2", 1, 2), ("hid", 4, 1), ("red1", 4, 2), ("cg", 1, 2), ("red2", 3, 2),
    ("gat2", 2, 2), ("out", 0, 0), ("out", 1, 0), ("gelu", 3, 2), ("out", 0, 1), ("red2", 4, 2), ("wt", 0, 2),
    ("cg", 2, 2), ("out", 1, 1), ("rs2", 0, 2), ("gat2", 3, 0), ("out", 2, 0), ("gelu", 4, 2), ("gat2", 3, 1),
    ("wt", 1, 2), ("out", 2, 1), ("cg", 3, 0), ("rs2", 1, 2), ("gat2", 4, 0), ("out", 3, 0), ("cg", 3, 1),
    ("gat2", 4, 1), ("rs2", 2, 2), ("out", 3, 1), ("cg", 4, 0), ("fin", 0, 2), ("outa", 4, 0), ("wt", 2, 2),
    ("outb", 4, 0), ("fin", 1, 2), ("cg", 4, 1), ("outa", 4, 1), ("fin", 2, 2), ("outb", 4, 1), ("rs2", 3, 2),
    ("wt", 3, 2), ("rs2", 4, 0), ("rs2", 4, 1), ("wt", 4, 2), ("fin", 3, 2), ("fin", 4, 0), ("fin", 4, 1),
)


def dot(a, b, dims):
    return lax.dot_general(a, b, ((dims[:1], dims[1:]), ((), ())), preferred_element_type=F32)


def body(
    x_hbm, g_hbm, w_in_hbm, w_out_hbm, b_in_hbm, b_out_hbm,
    out_o, out_i, w1g, out_b1, w2g, out_b2,
    xg, w_in, w_out, snd, crv, own, s, r1b, r2b, act, part, rab, sab, tab, b1g, b2g, b_in, b_out,
    load_sem, send_sem, ce_s, ag1_r, ag2_r, ce_r, y_r, gc_r, rs1_r, rs2_r,
):
    row, col = lax.axis_index("row"), lax.axis_index("col")
    y, core = row // 2, row % 2
    z, x = col // 4, col % 4
    abit, bbit = ((y + 1) // 2) % 2, y // 2
    ya, yb = y + 1 - 2 * (y % 2), 3 - y
    pair_a, pair_b = (ya * 2 + core, col), (yb * 2 + core, col)
    mate = (y * 2 + 1 - core, col)

    def zx(dz, dx):
        return (row, ((z + dz) % 4) * 4 + (x + dx) % 4)

    loads = [
        pltpu.make_async_copy(x_hbm, xg.at[:, 0, z, x], load_sem.at[0]),
        pltpu.make_async_copy(g_hbm, xg.at[:, 1, z, x], load_sem.at[1]),
        pltpu.make_async_copy(w_in_hbm, w_in, load_sem.at[2]),
        pltpu.make_async_copy(w_out_hbm, w_out, load_sem.at[3]),
        pltpu.make_async_copy(b_in_hbm, b_in, load_sem.at[4]),
        pltpu.make_async_copy(b_out_hbm, b_out, load_sem.at[5]),
    ]
    barrier = pltpu.get_barrier_semaphore()
    peers = [pair_a, pair_b, mate] + [zx(0, d) for d in (1, 2, 3)] + [zx(d, 0) for d in (1, 2, 3)]
    for p in peers:
        pl.semaphore_signal(barrier, inc=1, device_id=p, device_id_type=MESH)
    for cp in loads:
        cp.start()
    pl.semaphore_wait(barrier, len(peers))
    loads[0].wait()
    loads[1].wait()

    def rcopy(src, dst, ss, rs, dev):
        return lambda: pltpu.make_async_remote_copy(
            src_ref=src, dst_ref=dst, send_sem=ss, recv_sem=rs, device_id=dev, device_id_type=MESH
        ).start()

    lo, hi = pl.ds(0, DH), pl.ds(DH, DH)

    def ag1(c, t):
        rs = ag1_r.at[c, t]
        res = []
        for d in (1, 2, 3):
            ref = xg.at[c, t, z, x, :, lo]
            res.append(rcopy(ref, ref, send_sem.at[0], rs, zx(0, d)))
            ref = xg.at[c, t, z, x, :, hi]
            res.append(rcopy(ref, ref, send_sem.at[0], rs, zx(d, 0)))
        return res, xg.at[c, t, 0, 0:3], rs

    def ag2(c, t):
        rs = ag2_r.at[c, t]
        res = []
        for d in (1, 2, 3):
            ref = xg.at[c, t, z, :, :, lo]
            res.append(rcopy(ref, ref, send_sem.at[1], rs, zx(d, 0)))
            ref = xg.at[c, t, :, x, :, hi]
            res.append(rcopy(ref, ref, send_sem.at[1], rs, zx(0, d)))
        return res, xg.at[c, t, 0:3], rs

    def core_swap(c, t):
        rs = ce_r.at[c, t]
        return [rcopy(snd.at[t], crv.at[c, t], ce_s.at[t], rs, mate)], crv.at[c, t], rs

    def rows(start, n):
        return pl.ds(pl.multiple_of(start, TB), n)

    a_keep, a_send = abit * 32, (1 - abit) * 32
    b_keep, b_send = 64 + bbit * 32, 64 + (1 - bbit) * 32
    a_own, a_send2 = a_keep + bbit * 16, a_keep + (1 - bbit) * 16
    b_own, b_send2 = b_keep + abit * 16, b_keep + (1 - abit) * 16

    def pick(t):
        return slice(None) if t == 2 else t

    def parts(t):
        return (0, 1) if t == 2 else (t,)

    def sent_as(name, c, t):
        return (2,) if (name, c, 2) in SCHEDULE else parts(t)

    def y_red1(c, t):
        ss, rs = send_sem.at[2], y_r.at[c, t % 2, 0]
        t = pick(t)
        return [
            rcopy(s.at[c, t, rows(a_send, 32)], r1b.at[c, t, 0], ss, rs, pair_a),
            rcopy(s.at[c, t, rows(b_send, 32)], r1b.at[c, t, 1], ss, rs, pair_b),
        ], r1b.at[c, t], rs

    def y_red2(c, t):
        ss, rs = send_sem.at[3], y_r.at[c, t % 2, 1]
        t = pick(t)
        return [
            rcopy(s.at[c, t, rows(a_send2, 16)], r2b.at[c, t, 0], ss, rs, pair_b),
            rcopy(s.at[c, t, rows(b_send2, 16)], r2b.at[c, t, 1], ss, rs, pair_a),
        ], r2b.at[c, t], rs

    def y_gat1(c):
        ss, rs = send_sem.at[4], y_r.at[c, 0, 2]
        ref_a = act.at[c, :, rows(core * HALF + a_own, 16)]
        ref_b = act.at[c, :, rows(core * HALF + b_own, 16)]
        return [rcopy(ref_a, ref_a, ss, rs, pair_b), rcopy(ref_b, ref_b, ss, rs, pair_a)], act.at[c, :, 0:32], rs

    def y_gat2(c, t):
        ss, rs = send_sem.at[5], y_r.at[c, t % 2, 3]
        t = pick(t)
        ref_a = act.at[c, t, rows(core * HALF + a_keep, 32)]
        ref_b = act.at[c, t, rows(core * HALF + b_keep, 32)]
        return [rcopy(ref_a, ref_a, ss, rs, pair_a), rcopy(ref_b, ref_b, ss, rs, pair_b)], act.at[c, t, 0:64], rs

    def core_gat(c, t):
        rs = gc_r.at[c, t % 2]
        t = pick(t)
        ref = act.at[c, t, rows(core * HALF, HALF)]
        return [rcopy(ref, ref, send_sem.at[6], rs, mate)], act.at[c, t, 0:HALF], rs

    def rs1(c, t):
        ss, rs = send_sem.at[7], rs1_r.at[c, t]
        res = []
        for d in (1, 2, 3):
            src = part.at[c, t, :, (x + d) % 4, :, lo]
            res.append(rcopy(src, rab.at[c, t, 0, d - 1], ss, rs, zx(0, d)))
            src = part.at[c, t, (z + d) % 4, :, :, hi]
            res.append(rcopy(src, rab.at[c, t, 1, d - 1], ss, rs, zx(d, 0)))
        return res, rab.at[c, t], rs

    def rs1_half(c, t, which):
        ss, rs = send_sem.at[7], rs1_r.at[c, t]
        z_two = pl.ds(2 * which, 2)
        for d in (1, 2, 3):
            src = part.at[c, t, z_two, (x + d) % 4, :, lo]
            rcopy(src, rab.at[c, t, 0, d - 1, z_two], ss, rs, zx(0, d))()
            src = part.at[c, t, (z + d) % 4, :, :, hi]
            pl.when((z + d) % 4 // 2 == which)(rcopy(src, rab.at[c, t, 1, d - 1], ss, rs, zx(d, 0)))

    def rs2(c, t):
        ss, rs = send_sem.at[8], rs2_r.at[c, t % 2]
        t = pick(t)
        res = []
        for d in (1, 2, 3):
            src = sab.at[c, 0, t, (z + d) % 4]
            res.append(rcopy(src, tab.at[c, 0, d - 1, t], ss, rs, zx(d, 0)))
            src = sab.at[c, 1, t, (x + d) % 4]
            res.append(rcopy(src, tab.at[c, 1, d - 1, t], ss, rs, zx(0, d)))
        return res, tab.at[c, :, :, t], rs

    def start(stage):
        for send in stage[0]:
            send()

    def wait_bytes(size, sem):
        pltpu.make_async_copy(size, size, sem).wait()

    def wait(stage):
        wait_bytes(*stage[1:])

    def half_of(c, t, which):
        return xg[c, t, pl.ds(2 * which, 2)].reshape(HALF, DL)

    def chunk_of(c, t):
        return xg[c, t].reshape(ROWS, DL)

    def ag1_stage(c, t):
        start(ag1(c, t))

    def ag2_stage(c, t):
        wait(ag1(c, t))
        start(ag2(c, t))

    def hidden_stage(c, t):
        if c == 0:
            loads[2 + t].wait()
            loads[4 + t].wait()
        wait(ag2(c, t))
        lhs = jnp.concatenate([half_of(c, t, 1 - core), half_of(c, t, core)], axis=0)
        for n in range(0, FL, 512):
            if t == 0:
                r = dot(lhs, w_in[:, n:n + 512], (1, 0))
            else:
                r = dot(lhs, w_out[n:n + 512, :], (1, 1))
            snd[t, :, n:n + 512] = r[:HALF].astype(BF16)
            own[t, :, n:n + 512] = r[HALF:]
        start(core_swap(c, t))

    def red1_stage(c, t):
        for p in parts(t):
            wait(core_swap(c, p))
            wait_bytes(snd.at[p], ce_s.at[p])
            s[c, p] = (own[p] + crv[c, p].astype(F32)).astype(BF16)
        start(y_red1(c, t))

    def red2_stage(c, t):
        for p in sent_as("red1", c, t):
            wait(y_red1(c, p))
        for p in parts(t):
            for k, keep in ((0, a_keep), (1, b_keep)):
                here = s.at[c, p, rows(keep, 32)]
                here[...] = (here[...].astype(F32) + r1b[c, p, k].astype(F32)).astype(BF16)
        start(y_red2(c, t))

    def gelu_stage(c, _):
        for p in sent_as("red2", c, 2):
            wait(y_red2(c, p))
        for k, mine in ((0, a_own), (1, b_own)):
            total = s[c, :, rows(mine, 16)].astype(F32) + r2b[c, :, k].astype(F32)
            hidden = total[0] + b_in[...][None]
            half = 0.5 * (1.0 + lax.erf(hidden * 0.7071067811865476))
            slope = half + hidden * jnp.exp(-0.5 * hidden * hidden) * 0.3989422804014327
            at = rows(core * HALF + mine, 16)
            act[c, 0, at] = (hidden * half).astype(BF16)
            act[c, 1, at] = (total[1] * slope).astype(BF16)
        start(y_gat1(c))

    def gat2_stage(c, t):
        if t != 1:
            wait(y_gat1(c))
        start(y_gat2(c, t))

    def core_gat_stage(c, t):
        wait(y_gat2(c, t))
        start(core_gat(c, t))

    def out_stage(c, t):
        if t in sent_as("cg", c, t):
            wait(core_gat(c, t))
        elif t == 0:
            wait(core_gat(c, 2))
        for n in range(0, DL, 256):
            if t == 0:
                r = dot(act[c, 0], w_out[:, n:n + 256], (1, 0))
            else:
                r = dot(act[c, 1], w_in[n:n + 256, :], (1, 1))
            part[c, t, :, :, :, n:n + 256] = r.astype(BF16).reshape(4, 4, TB, 256)
        start(rs1(c, t))

    def out_half(c, t, which):
        at = rows(which * HALF, HALF)
        for n in range(0, DL, 256):
            if t == 0:
                r = dot(act[c, 0, at], w_out[:, n:n + 256], (1, 0))
            else:
                r = dot(act[c, 1, at], w_in[n:n + 256, :], (1, 1))
            part[c, t, pl.ds(2 * which, 2), :, :, n:n + 256] = r.astype(BF16).reshape(2, 4, TB, 256)
        rs1_half(c, t, which)

    def out_own_stage(c, t):
        out_half(c, t, core)

    def out_other_stage(c, t):
        if t in sent_as("cg", c, t):
            wait(core_gat(c, t))
        elif t == 0:
            wait(core_gat(c, 2))
        out_half(c, t, 1 - core)

    def rs2_stage(c, t):
        for p in parts(t):
            wait(rs1(c, p))
            total = part[c, p, :, x, :, lo].astype(F32)
            for d in range(3):
                total += rab[c, p, 0, d].astype(F32)
            sab[c, 0, p] = total.astype(BF16)
            total = part[c, p, z, :, :, hi].astype(F32)
            for d in range(3):
                total += rab[c, p, 1, d].astype(F32)
            sab[c, 1, p] = total.astype(BF16)
        start(rs2(c, t))

    def final_stage(c, t):
        wait(rs2(c, t))
        for k, me, cols in ((0, z, lo), (1, x, hi)):
            for p in parts(t):
                total = sab[c, k, p, me].astype(F32)
                for d in range(3):
                    total += tab[c, k, d, p].astype(F32)
                if p == 0:
                    out_o[c, :, cols] = (total + b_out[cols][None]).astype(BF16)
                else:
                    out_i[c, :, cols] = total.astype(BF16)

    def weight_stage(c, _):
        def add(ref, at, value):
            ref[at] = value if c == 0 else ref[at] + value

        g_k = chunk_of(c, 1)
        for n in range(0, FL, 512):
            add(w2g, (slice(n, n + 512), slice(None)), dot(act[c, 0, :, n:n + 512], g_k, (0, 0)))
        x_k = chunk_of(c, 0)
        for n in range(0, FL, 512):
            add(w1g, (slice(None), slice(n, n + 512)), dot(x_k, act[c, 1, :, n:n + 512], (0, 0)))
        add(b1g, ..., jnp.sum(act[c, 1].astype(F32), axis=0, keepdims=True))
        add(b2g, ..., jnp.sum(g_k.astype(F32), axis=0, keepdims=True))
        if c == CH - 1:
            out_b1[...] = jnp.sum(b1g[...], axis=0)
            out_b2[...] = jnp.sum(b2g[...], axis=0)

    stages = dict(
        ag1=ag1_stage, ag2=ag2_stage, hid=hidden_stage, red1=red1_stage, red2=red2_stage, gelu=gelu_stage,
        gat2=gat2_stage, cg=core_gat_stage, out=out_stage,
        outa=out_own_stage, outb=out_other_stage, rs2=rs2_stage, fin=final_stage, wt=weight_stage,
    )
    for name, c, t in SCHEDULE:
        stages[name](c, t)

    sent = (
        xg.at[:, :, 0, 0:3], xg.at[:, :, 0:3], r1b, r2b, act.at[:, :, 0:32], act.at[:, :, 0:64],
        act.at[:, :, 0:HALF], rab, tab,
    )
    for k, size in enumerate(sent):
        wait_bytes(size, send_sem.at[k])


def write_out(*refs):
    sems = refs[-1]
    copies = [pltpu.make_async_copy(refs[k], refs[k + 6], sems.at[k]) for k in range(6)]
    for cp in copies:
        cp.start()
    for cp in copies:
        cp.wait()


def shards(inputs, w_in, b_in, w_out, b_out, out_grad):
    any_spec = pl.BlockSpec(memory_space=pl.ANY)
    vmem_spec = pl.BlockSpec(memory_space=pltpu.VMEM)
    dma = pltpu.SemaphoreType.DMA
    outs = pl.pallas_call(
        body,
        out_shape=[
            pltpu.VMEM((CH, TB, DL), BF16),
            pltpu.VMEM((CH, TB, DL), BF16),
            pltpu.VMEM((DL, FL), F32),
            pltpu.VMEM((FL,), F32),
            pltpu.VMEM((FL, DL), F32),
            pltpu.VMEM((DL,), F32),
        ],
        in_specs=[any_spec] * 6,
        out_specs=[vmem_spec] * 6,
        scratch_shapes=[
            pltpu.VMEM((CH, 2, 4, 4, TB, DL), BF16),
            pltpu.VMEM((DL, FL), BF16),
            pltpu.VMEM((FL, DL), BF16),
            pltpu.VMEM((2, HALF, FL), BF16),
            pltpu.VMEM((CH, 2, HALF, FL), BF16),
            pltpu.VMEM((2, HALF, FL), F32),
            pltpu.VMEM((CH, 2, HALF, FL), BF16),
            pltpu.VMEM((CH, 2, 2, 32, FL), BF16),
            pltpu.VMEM((CH, 2, 2, 16, FL), BF16),
            pltpu.VMEM((CH, 2, ROWS, FL), BF16),
            pltpu.VMEM((CH, 2, 4, 4, TB, DL), BF16),
            pltpu.VMEM((CH, 2, 2, 3, 4, TB, DH), BF16),
            pltpu.VMEM((CH, 2, 2, 4, TB, DH), BF16),
            pltpu.VMEM((CH, 2, 3, 2, TB, DH), BF16),
            pltpu.VMEM((1, FL), F32),
            pltpu.VMEM((1, DL), F32),
            pltpu.VMEM((FL,), F32),
            pltpu.VMEM((DL,), F32),
            dma((6,)),
            dma((9,)), dma((2,)),
            dma((CH, 2)), dma((CH, 2)), dma((CH, 2)), dma((CH, 2, 4)), dma((CH, 2)), dma((CH, 2)), dma((CH, 2)),
        ],
        compiler_params=pltpu.CompilerParams(
            collective_id=0, has_side_effects=True, vmem_limit_bytes=48 * 2**20
        ),
        cost_estimate=pl.CostEstimate(flops=18 * 10**9, bytes_accessed=15 * 10**6, transcendentals=10**6),
        name="mlp",
    )(
        inputs.reshape(CH, TB, DL), out_grad.reshape(CH, TB, DL), w_in, w_out,
        b_in, b_out,
    )
    outs = pl.pallas_call(
        write_out,
        out_shape=[jax.ShapeDtypeStruct(o.shape, o.dtype) for o in outs],
        in_specs=[vmem_spec] * 6,
        out_specs=[any_spec] * 6,
        scratch_shapes=[dma((6,))],
        compiler_params=pltpu.CompilerParams(vmem_limit_bytes=2**20),
        name="write_out",
    )(*[pltpu.with_memory_space_constraint(o, pltpu.VMEM) for o in outs])
    output, input_grad, *grads = outs
    return output.reshape(CH * TB, DL), input_grad.reshape(CH * TB, DL), *grads


def solution(mesh):
    placed = (
        P("col", "row"),
        P("row", "col"),
        P("col"),
        P("col", "row"),
        P("row"),
        P("col", "row"),
    )
    return jax.shard_map(
        shards,
        mesh=mesh,
        in_specs=placed,
        out_specs=(
            P("col", "row"),
            P("col", "row"),
            P("row", "col"),
            P("col"),
            P("col", "row"),
            P("row"),
        ),
        check_vma=False,
    )
```
